512 devices in a mesh: frame: 16 (over y, x_lo), row: 32 (over x_hi, z, core).
Axes of the slice: x: 4 (x_hi: 2, x_lo: 2; x = x_hi * 2 + x_lo), y: 8, z: 8, core: 2. Of those that a mesh axis runs over, the one named last changes fastest.
Arguments:
- queries: bfloat16 [16, 32, 128, 1536], P('frame', 'row'), may hold values from -100 to 100
- keys: bfloat16 [16, 32, 256, 1536], P('frame', 'row'), may hold values from -5 to 5
- values: bfloat16 [16, 32, 256, 1536], P('frame', 'row'), may hold values from -24 to 24
- pad_counts: int32 [16, 32], replicated, may hold values from 0 to 192, as said below
Outputs:
- attended: bfloat16 [16, 32, 128, 1536], P('frame', 'row')
The draws below stay inside these ranges and needn't reach their ends.
Inputs may be any that keep to these rules, and one draw needn't show every extreme that they name: `pad_counts`: each entry counts padded tokens of one tile; the value 3 * 64 and the value 0 each occur in every draw.
All inputs are finite; a program needn't handle non-finite values.
Results may differ from the reference program's by a relative error of at most 0.0049.
Values may be sent and summed in bfloat16 or wider, within the bound.
A program may use at most 64 MiB of HBM per device.

```python
import jax
import jax.numpy as jnp
from jax import lax

H = 12
HDIM = 128
TILE = 256
QROWS = 128
RT = 4
FT = 16
CT = 8


def key_base(key):
    return jnp.clip(jax.random.normal(key, (FT, RT * CT, TILE, H * HDIM), jnp.float32), -5.0, 5.0)


def draw_keys(key, part):
    base = key_base(key)
    return base.astype(jnp.bfloat16)


def draw_queries(key, part):
    key = jax.random.fold_in(key, 7)
    fresh = 2.0 * jnp.clip(jax.random.normal(key, (FT, RT * CT, QROWS, H * HDIM), jnp.float32), -5.0, 5.0)
    return fresh.astype(jnp.bfloat16)


def draw_pad_counts(key, part):
    key = jax.random.fold_in(key, 5)
    first, second, third = jax.random.split(key, 3)
    count = FT * RT * CT
    most = 3 * TILE // 4
    drawn = jax.random.randint(first, (count,), 0, most + 1, jnp.int32)
    lowest = jax.random.randint(second, (), 0, count, jnp.int32)
    stride = jax.random.randint(third, (), 1, count, jnp.int32)
    highest = (lowest + stride) % count
    drawn = drawn.at[lowest].set(0).at[highest].set(most)
    return drawn.reshape(FT, RT * CT)


def block_levels(key, dims, pieces, low, high):
    factor_of, own = 1.0, jax.random.fold_in(key, 6)
    for axis_at, parts in pieces:
        heights = jnp.exp(jax.random.uniform(jax.random.fold_in(own, axis_at), (parts,), jnp.float32, low / len(pieces), high / len(pieces)))
        factor_of = factor_of * jnp.repeat(heights, dims[axis_at] // parts).reshape([-1 if axis == axis_at else 1 for axis in range(len(dims))])
    return factor_of


def noise(stream_key, dims, deviation, most, shards=(), held_as=jnp.bfloat16):
    factor_of = block_levels(stream_key, dims, shards, -0.22, 0.18) if shards else 1.0
    values = jax.random.normal(stream_key, dims, jnp.float32) * deviation * factor_of
    return jnp.minimum(jnp.maximum(values, -most), most).astype(held_as)


def setup_inputs(seed: int = 0) -> dict:
    key_list = jax.random.split(jax.random.key(seed), 5)
    return {
        "queries": draw_queries(jax.random.fold_in(key_list[4], 71), 0),
        "keys": draw_keys(jax.random.fold_in(key_list[4], 71), 0),
        "values": noise(key_list[2], (FT, RT * CT, TILE, H * HDIM), 4.0, 24.0, ((0, 16), (1, 32))),
        "pad_counts": draw_pad_counts(jax.random.fold_in(key_list[4], 71), 0),
    }


def attend_stack(local_queries, near_pairs, near_pads):
    width = H * HDIM
    position = jnp.arange(TILE, dtype=jnp.int32)
    live = (position[None, None, :] < TILE - near_pads[..., None]).reshape(-1)
    flat_pairs = near_pairs.reshape(-1, 2 * width)
    scale = HDIM ** -0.5

    def one_head(head):
        query_head = lax.dynamic_slice_in_dim(local_queries, head * HDIM, HDIM, 1)
        key_head = lax.dynamic_slice_in_dim(flat_pairs, head * HDIM, HDIM, 1)
        value_head = lax.dynamic_slice_in_dim(flat_pairs, width + head * HDIM, HDIM, 1)
        scores = lax.dot_general(query_head, key_head, (((1,), (1,)), ((), ())), preferred_element_type=jnp.float32) * scale
        scores = jnp.where(live[None, :], scores, jnp.float32(-1e30))
        top_score = jnp.max(scores, axis=1, keepdims=True)
        expo = jnp.exp(scores - top_score)
        total = jnp.sum(expo, axis=1, keepdims=True)
        weights = (expo / total).astype(jnp.bfloat16)
        return jnp.dot(weights, value_head, preferred_element_type=jnp.float32)

    heads_out = lax.map(one_head, jnp.arange(H, dtype=jnp.int32))
    rows = local_queries.shape[0]
    return jnp.transpose(heads_out, (1, 0, 2)).reshape(rows, width).astype(jnp.bfloat16)


def reference(queries, keys, values, pad_counts):
    width = H * HDIM
    pairs = jnp.concatenate((keys, values), axis=-1).reshape(FT, RT, CT, TILE, 2 * width)
    padded_pairs = jnp.pad(pairs, ((1, 1), (1, 1), (0, 0), (0, 0), (0, 0)))
    padded_pads = jnp.pad(pad_counts.reshape(FT, RT, CT), ((1, 1), (1, 1), (0, 0)), constant_values=TILE)

    def one_stack(flat_index):
        frame_index = (flat_index // (RT * CT)).astype(jnp.int32)
        row_index = (flat_index % (RT * CT)).astype(jnp.int32)
        row_tile = (row_index // CT).astype(jnp.int32)
        column_tile = (row_index % CT).astype(jnp.int32)
        zero = jnp.int32(0)
        near_pairs = lax.dynamic_slice(padded_pairs, (frame_index, row_tile, column_tile, zero, zero), (3, 3, 1, TILE, 2 * width)).reshape(3, 3, TILE, 2 * width)
        near_pads = lax.dynamic_slice(padded_pads, (frame_index, row_tile, column_tile), (3, 3, 1)).reshape(3, 3)
        local_queries = queries[frame_index, row_index]
        return attend_stack(local_queries, near_pairs, near_pads)

    stacks = lax.map(one_stack, jnp.arange(FT * RT * CT, dtype=jnp.int32))
    return stacks.reshape(FT, RT * CT, QROWS, width)
```

```python
import functools

import jax
import jax.numpy as jnp
from jax import lax
from jax.experimental import pallas as pl
from jax.experimental.pallas import tpu as pltpu
from jax.sharding import PartitionSpec as P

HDIM = 128
TILE = 256
QROWS = 128
RT = 4
LOG2E = 1.4426950408889634
DEAD = -1e30
AHEAD = 4
STAT = 16

KV_X, KV_Y, Q_P, Q_X, O_P, O_X = range(6)


def split3(row):
    high = row.astype(jnp.bfloat16).astype(jnp.float32)
    rest = row - high
    middle = rest.astype(jnp.bfloat16).astype(jnp.float32)
    return high, middle, rest - middle


def packed_stats(top, total):
    rows = split3(top) + split3(total)
    at = lax.broadcasted_iota(jnp.int32, (STAT, top.shape[1]), 0)
    out = jnp.zeros((STAT, top.shape[1]), jnp.float32)
    for i, row in enumerate(rows):
        out = jnp.where(at == i, row, out)
    return out.astype(jnp.bfloat16)


def kernel(
    heads, columns, frames, q_hbm, k_hbm, v_hbm, pads, out, kv, qb, part, part_stat,
    to_p, to_x, from_p, from_x, local_sem, send_sem, recv_sem,
):
    scale = HDIM ** (-0.5) * LOG2E
    frame, row = lax.axis_index("frame"), lax.axis_index("row")
    rows = RT * columns
    half = 2 * columns
    even = lax.rem(frame, 2) == 0
    r = row // columns
    inner = jnp.logical_or(r == 1, r == 2)
    other_frame = jnp.where(even, frame + 1, frame - 1)
    far_frame = jnp.where(even, frame - 1, frame + 1)
    ahead_frame = lax.rem(jnp.where(even, frame + 2, frame + frames - 2), frames)
    behind_frame = lax.rem(jnp.where(even, frame + frames - 2, frame + 2), frames)
    p_row = (row // half) * half + lax.rem(lax.rem(row, half) + columns, half)
    x_row = lax.rem(row + half, rows)

    across = (other_frame, row)
    onward = (ahead_frame, row)
    side = (frame, p_row)
    cross = (frame, x_row)

    def local(h):
        cut = pl.ds(pl.multiple_of(h * HDIM, HDIM), HDIM)
        return (
            pltpu.make_async_copy(q_hbm.at[0, 0, :, cut], qb.at[h, pl.ds(0, QROWS)], local_sem.at[0, h]),
            pltpu.make_async_copy(k_hbm.at[0, 0, :, cut], kv.at[0, h, pl.ds(0, TILE)], local_sem.at[1, h]),
            pltpu.make_async_copy(v_hbm.at[0, 0, :, cut], kv.at[0, h, pl.ds(TILE, TILE)], local_sem.at[2, h]),
        )

    def remote(kind, h):
        src, dst, device = {
            KV_X: lambda: (kv.at[0, h], kv.at[1, h], across),
            KV_Y: lambda: (kv.at[1, h], kv.at[2, h], onward),
            Q_P: lambda: (qb.at[h, pl.ds(0, QROWS)], qb.at[h, pl.ds(QROWS, QROWS)], side),
            Q_X: lambda: (qb.at[h, pl.ds(QROWS, QROWS)], qb.at[h, pl.ds(2 * QROWS, QROWS)], cross),
            O_P: lambda: (to_p.at[h], from_p.at[h], side),
            O_X: lambda: (to_x.at[h], from_x.at[h], cross),
        }[kind]()
        return pltpu.make_async_remote_copy(
            src_ref=src, dst_ref=dst, send_sem=send_sem.at[kind, h], recv_sem=recv_sem.at[kind, h],
            device_id=device, device_id_type=pl.DeviceIdType.MESH,
        )

    @pl.loop(0, heads)
    def _(h):
        for copy in local(h):
            copy.start()

    barrier = pltpu.get_barrier_semaphore()
    for device in (across, onward, (behind_frame, row), side, cross):
        pl.semaphore_signal(barrier, inc=1, device_id=device, device_id_type=pl.DeviceIdType.MESH)

    live0 = TILE - pads[frame, row]
    live1 = TILE - pads[other_frame, row]
    far_there = jnp.logical_and(far_frame >= 0, far_frame < frames)
    live2 = jnp.where(far_there, TILE - pads[jnp.clip(far_frame, 0, frames - 1), row], 0)
    lives = (live0, live1, live2)

    pl.semaphore_wait(barrier, 5)

    def send_own(h):
        for copy in local(h):
            copy.wait()
        remote(Q_P, h).start()
        remote(KV_X, h).start()

    def attend(h, queries):
        at = lax.broadcasted_iota(jnp.int32, (TILE, queries.shape[0]), 0)
        scores = []
        for slot in range(3):
            s = lax.dot_general(
                kv[slot, h, 0:TILE], queries, (((1,), (1,)), ((), ())), preferred_element_type=jnp.float32
            )
            scores.append(jnp.where(at < lives[slot], s, DEAD))
        top = functools.reduce(jnp.maximum, [jnp.max(s, axis=0, keepdims=True) for s in scores])
        total, acc = 0.0, 0.0
        for slot in range(3):
            expo = jnp.exp2((scores[slot] - top) * scale)
            total = total + jnp.sum(expo, axis=0, keepdims=True)
            acc = acc + lax.dot_general(
                kv[slot, h, TILE:2 * TILE], expo.astype(jnp.bfloat16), (((0,), (0,)), ((), ())),
                preferred_element_type=jnp.float32,
            )
        return acc, top, total

    def packed_into(ref, h, acc, top, total):
        ref[h, 0:HDIM] = acc.astype(jnp.bfloat16)
        ref[h, HDIM:HDIM + STAT] = packed_stats(top, total)

    def keep(which, h, acc, top, total):
        part[which, h] = acc
        part_stat[which, h, 0:1] = top
        part_stat[which, h, 1:2] = total

    def merged(which, h, ref):
        stats = ref[h, HDIM:HDIM + STAT].astype(jnp.float32)
        top2 = stats[0:1] + stats[1:2] + stats[2:3]
        total2 = stats[3:4] + stats[4:5] + stats[5:6]
        top1, total1 = part_stat[which, h, 0:1], part_stat[which, h, 1:2]
        top = jnp.maximum(top1, top2)
        w1, w2 = jnp.exp2((top1 - top) * scale), jnp.exp2((top2 - top) * scale)
        acc = part[which, h] * w1 + ref[h, 0:HDIM].astype(jnp.float32) * w2
        return acc, top, total1 * w1 + total2 * w2

    @pl.loop(0, min(AHEAD, heads))
    def _(h):
        send_own(h)

    @pl.loop(0, heads + 3)
    def _(t):
        @pl.when(t + AHEAD < heads)
        def _():
            send_own(t + AHEAD)

        @pl.when(t < heads)
        def _():
            remote(Q_P, t).wait_recv()

            @pl.when(jnp.logical_not(inner))
            def _():
                remote(Q_X, t).start()

            remote(KV_X, t).wait_recv()
            remote(KV_Y, t).start()

        @pl.when(jnp.logical_and(t >= 1, t < heads + 1))
        def _():
            h = t - 1
            remote(KV_Y, h).wait_recv()

            @pl.when(inner)
            def _():
                remote(Q_X, h).wait_recv()
                packed_into(to_x, h, *attend(h, qb[h, 2 * QROWS:3 * QROWS]))
                remote(O_X, h).start()

            acc, top, total = attend(h, qb[h, 0:2 * QROWS])
            keep(0, h, acc[:, 0:QROWS], top[:, 0:QROWS], total[:, 0:QROWS])
            for_p = acc[:, QROWS:], top[:, QROWS:], total[:, QROWS:]

            @pl.when(inner)
            def _():
                packed_into(to_p, h, *for_p)
                remote(O_P, h).start()

            @pl.when(jnp.logical_not(inner))
            def _():
                keep(1, h, *for_p)

        @pl.when(jnp.logical_and(jnp.logical_not(inner), jnp.logical_and(t >= 2, t < heads + 2)))
        def _():
            h = t - 2
            remote(O_X, h).wait_recv()
            packed_into(to_p, h, *merged(1, h, from_x))
            remote(O_P, h).start()

        @pl.when(t >= 3)
        def _():
            h = t - 3
            remote(O_P, h).wait_recv()
            acc, top, total = merged(0, h, from_p)
            done = jnp.transpose(acc / total)
            out[0, 0, :, pl.ds(pl.multiple_of(h * HDIM, HDIM), HDIM)] = done.astype(out.dtype)

    @pl.loop(0, heads)
    def _(h):
        for kind in (KV_X, KV_Y, Q_P, O_P):
            remote(kind, h).wait_send()

        @pl.when(inner)
        def _():
            remote(O_X, h).wait_send()

        @pl.when(jnp.logical_not(inner))
        def _():
            remote(Q_X, h).wait_send()


def shards(queries, keys, values, pad_counts):
    width = queries.shape[-1]
    heads = width // HDIM
    frames, rows = pad_counts.shape
    bf16 = jnp.bfloat16
    return pl.pallas_call(
        functools.partial(kernel, heads, rows // RT, frames),
        out_shape=jax.ShapeDtypeStruct(queries.shape, bf16),
        in_specs=[pl.BlockSpec(memory_space=pl.ANY)] * 3 + [pl.BlockSpec(memory_space=pltpu.SMEM)],
        out_specs=pl.BlockSpec(memory_space=pltpu.VMEM),
        scratch_shapes=[
            pltpu.VMEM((3, heads, 2 * TILE, HDIM), bf16),
            pltpu.VMEM((heads, 3 * QROWS, HDIM), bf16),
            pltpu.VMEM((2, heads, HDIM, QROWS), jnp.float32),
            pltpu.VMEM((2, heads, 8, QROWS), jnp.float32),
        ]
        + [pltpu.VMEM((heads, HDIM + STAT, QROWS), bf16)] * 4
        + [
            pltpu.SemaphoreType.DMA((3, heads)),
            pltpu.SemaphoreType.DMA((6, heads)),
            pltpu.SemaphoreType.DMA((6, heads)),
        ],
        compiler_params=pltpu.CompilerParams(
            collective_id=0, has_side_effects=True, vmem_limit_bytes=40 * 1024 * 1024
        ),
    )(queries, keys, values, pad_counts)


def solution(mesh):
    spec = P("frame", "row", None, None)
    return jax.shard_map(
        shards, mesh=mesh, in_specs=(spec, spec, spec, P()), out_specs=spec, check_vma=False
    )
```

```python
import functools

import jax
import jax.numpy as jnp
from jax import lax
from jax.experimental import pallas as pl
from jax.experimental.pallas import tpu as pltpu
from jax.sharding import PartitionSpec as P

HDIM = 128
TILE = 256
QROWS = 128
RT = 4
LOG2E = 1.4426950408889634
AHEAD = 4
LAG = 2
STAT = 16

KV_X, KV_Y, Q_P, Q_X, O_P, O_X = range(6)


def split3(row):
    high = row.astype(jnp.bfloat16).astype(jnp.float32)
    rest = row - high
    middle = rest.astype(jnp.bfloat16).astype(jnp.float32)
    return high, middle, rest - middle


def packed_stats(top, total):
    rows = split3(top) + split3(total)
    at = lax.broadcasted_iota(jnp.int32, (STAT, top.shape[1]), 0)
    out = jnp.zeros((STAT, top.shape[1]), jnp.float32)
    for i, row in enumerate(rows):
        out = jnp.where(at == i, row, out)
    return out.astype(jnp.bfloat16)


def kernel(
    heads, columns, frames, q_hbm, k_hbm, v_hbm, pads, out, kv, qb, part, part_stat,
    to_p, to_x, from_p, from_x, raw_k, raw_v, live_rows, local_sem, send_sem, recv_sem,
):
    scale = HDIM ** (-0.5) * LOG2E
    frame, row = lax.axis_index("frame"), lax.axis_index("row")
    rows = RT * columns
    half = 2 * columns
    even = lax.rem(frame, 2) == 0
    r = row // columns
    inner = jnp.logical_or(r == 1, r == 2)
    other_frame = jnp.where(even, frame + 1, frame - 1)
    far_frame = jnp.where(even, frame - 1, frame + 1)
    ahead_frame = lax.rem(jnp.where(even, frame + 2, frame + frames - 2), frames)
    behind_frame = lax.rem(jnp.where(even, frame + frames - 2, frame + 2), frames)
    p_row = (row // half) * half + lax.rem(lax.rem(row, half) + columns, half)
    x_row = lax.rem(row + half, rows)

    across = (other_frame, row)
    onward = (ahead_frame, row)
    side = (frame, p_row)
    cross = (frame, x_row)

    def local(h):
        cut = pl.ds(pl.multiple_of(h * HDIM, HDIM), HDIM)
        return (
            pltpu.make_async_copy(q_hbm.at[0, 0, :, cut], qb.at[h, pl.ds(0, QROWS)], local_sem.at[0, h]),
            pltpu.make_async_copy(k_hbm.at[0, 0, :, cut], raw_k.at[h], local_sem.at[1, h]),
            pltpu.make_async_copy(v_hbm.at[0, 0, :, cut], raw_v.at[h], local_sem.at[2, h]),
        )

    def remote(kind, h):
        src, dst, device = {
            KV_X: lambda: (kv.at[0, h], kv.at[1, h], across),
            KV_Y: lambda: (kv.at[1, h], kv.at[2, h], onward),
            Q_P: lambda: (qb.at[h, pl.ds(0, QROWS)], qb.at[h, pl.ds(QROWS, QROWS)], side),
            Q_X: lambda: (qb.at[h, pl.ds(QROWS, QROWS)], qb.at[h, pl.ds(2 * QROWS, QROWS)], cross),
            O_P: lambda: (to_p.at[h], from_p.at[h], side),
            O_X: lambda: (to_x.at[h], from_x.at[h], cross),
        }[kind]()
        return pltpu.make_async_remote_copy(
            src_ref=src, dst_ref=dst, send_sem=send_sem.at[kind, h], recv_sem=recv_sem.at[kind, h],
            device_id=device, device_id_type=pl.DeviceIdType.MESH,
        )

    @pl.loop(0, heads)
    def _(h):
        for copy in local(h):
            copy.start()

    barrier = pltpu.get_barrier_semaphore()
    for device in (across, onward, (behind_frame, row), side, cross):
        pl.semaphore_signal(barrier, inc=1, device_id=device, device_id_type=pl.DeviceIdType.MESH)

    live0 = TILE - pads[frame, row]
    live1 = TILE - pads[other_frame, row]
    far_there = jnp.logical_and(far_frame >= 0, far_frame < frames)
    live2 = jnp.where(far_there, TILE - pads[jnp.clip(far_frame, 0, frames - 1), row], 0)
    lane = lax.broadcasted_iota(jnp.int32, (STAT, TILE), 1)
    for slot, live in enumerate((live0, live1, live2)):
        live_rows[slot] = jnp.where(lane < live, 1.0, 0.0).astype(jnp.bfloat16)

    pl.semaphore_wait(barrier, 5)

    def send_own(h):
        copies = local(h)
        copies[0].wait()
        remote(Q_P, h).start()
        copies[1].wait()
        copies[2].wait()
        at = lax.broadcasted_iota(jnp.int32, (TILE, HDIM), 0)
        keys = raw_k[h].astype(jnp.float32)
        kv[0, h, 0:TILE] = jnp.where(at < live0, keys, keys[0:1]).astype(jnp.bfloat16)
        values = jnp.where(at < live0, raw_v[h].astype(jnp.float32), 0.0)
        for i in range(TILE // HDIM):
            block = jnp.transpose(values[i * HDIM:(i + 1) * HDIM])
            kv[0, h, TILE + i * HDIM:TILE + (i + 1) * HDIM] = block.astype(jnp.bfloat16)
        remote(KV_X, h).start()

    def attend(h, queries):
        scores = [
            lax.dot_general(
                kv[slot, h, 0:TILE], queries, (((1,), (1,)), ((), ())), preferred_element_type=jnp.float32
            )
            for slot in range(3)
        ]
        top = functools.reduce(jnp.maximum, [jnp.max(s, axis=0, keepdims=True) for s in scores])
        expo = jnp.concatenate([jnp.exp2((s - top) * scale).astype(jnp.bfloat16) for s in scores], axis=0)
        turned = jnp.concatenate(
            [kv[slot, h, TILE + i * HDIM:TILE + (i + 1) * HDIM] for slot in range(3) for i in range(TILE // HDIM)],
            axis=1,
        )
        alive = jnp.concatenate([live_rows[slot] for slot in range(3)], axis=1)
        both = jnp.dot(jnp.concatenate([turned, alive], axis=0), expo, preferred_element_type=jnp.float32)
        return both[0:HDIM], top, both[HDIM:HDIM + 1]

    def packed_into(ref, h, acc, top, total):
        ref[h, 0:HDIM] = acc.astype(jnp.bfloat16)
        ref[h, HDIM:HDIM + STAT] = packed_stats(top, total)

    def keep(which, h, acc, top, total):
        part[which, h] = acc
        part_stat[which, h, 0:1] = top
        part_stat[which, h, 1:2] = total

    def merged(which, h, ref):
        stats = ref[h, HDIM:HDIM + STAT].astype(jnp.float32)
        top2 = stats[0:1] + stats[1:2] + stats[2:3]
        total2 = stats[3:4] + stats[4:5] + stats[5:6]
        top1, total1 = part_stat[which, h, 0:1], part_stat[which, h, 1:2]
        top = jnp.maximum(top1, top2)
        w1, w2 = jnp.exp2((top1 - top) * scale), jnp.exp2((top2 - top) * scale)
        acc = part[which, h] * w1 + ref[h, 0:HDIM].astype(jnp.float32) * w2
        return acc, top, total1 * w1 + total2 * w2

    @pl.loop(0, min(AHEAD, heads))
    def _(h):
        send_own(h)

    def within(at):
        return jnp.logical_and(at >= 0, at < heads)

    @pl.loop(0, heads + 3 * LAG)
    def _(t):
        @pl.when(t + AHEAD < heads)
        def _():
            send_own(t + AHEAD)

        @pl.when(t < heads)
        def _():
            remote(Q_P, t).wait_recv()

            @pl.when(jnp.logical_not(inner))
            def _():
                remote(Q_X, t).start()

            remote(KV_X, t).wait_recv()
            remote(KV_Y, t).start()

        @pl.when(within(t - LAG))
        def _():
            h = t - LAG
            remote(KV_Y, h).wait_recv()

            @pl.when(jnp.logical_not(far_there))
            def _():
                kv[2, h, 0:TILE] = kv[0, h, 0:TILE]
                kv[2, h, TILE:2 * TILE] = jnp.zeros((TILE, HDIM), jnp.bfloat16)

            @pl.when(inner)
            def _():
                remote(Q_X, h).wait_recv()
                packed_into(to_x, h, *attend(h, qb[h, 2 * QROWS:3 * QROWS]))
                remote(O_X, h).start()

            acc, top, total = attend(h, qb[h, 0:2 * QROWS])
            keep(0, h, acc[:, 0:QROWS], top[:, 0:QROWS], total[:, 0:QROWS])
            for_p = acc[:, QROWS:], top[:, QROWS:], total[:, QROWS:]

            @pl.when(inner)
            def _():
                packed_into(to_p, h, *for_p)
                remote(O_P, h).start()

            @pl.when(jnp.logical_not(inner))
            def _():
                keep(1, h, *for_p)

        @pl.when(jnp.logical_and(jnp.logical_not(inner), within(t - 2 * LAG)))
        def _():
            h = t - 2 * LAG
            remote(O_X, h).wait_recv()
            packed_into(to_p, h, *merged(1, h, from_x))
            remote(O_P, h).start()

        @pl.when(t >= 3 * LAG)
        def _():
            h = t - 3 * LAG
            remote(O_P, h).wait_recv()
            acc, top, total = merged(0, h, from_p)
            done = jnp.transpose(acc / total)
            out[0, 0, :, pl.ds(pl.multiple_of(h * HDIM, HDIM), HDIM)] = done.astype(out.dtype)

    @pl.loop(0, heads)
    def _(h):
        for kind in (KV_X, KV_Y, Q_P, O_P):
            remote(kind, h).wait_send()

        @pl.when(inner)
        def _():
            remote(O_X, h).wait_send()

        @pl.when(jnp.logical_not(inner))
        def _():
            remote(Q_X, h).wait_send()


def shards(queries, keys, values, pad_counts):
    width = queries.shape[-1]
    heads = width // HDIM
    frames, rows = pad_counts.shape
    bf16 = jnp.bfloat16
    return pl.pallas_call(
        functools.partial(kernel, heads, rows // RT, frames),
        out_shape=jax.ShapeDtypeStruct(queries.shape, bf16),
        in_specs=[pl.BlockSpec(memory_space=pl.ANY)] * 3 + [pl.BlockSpec(memory_space=pltpu.SMEM)],
        out_specs=pl.BlockSpec(memory_space=pltpu.VMEM),
        scratch_shapes=[
            pltpu.VMEM((3, heads, 2 * TILE, HDIM), bf16),
            pltpu.VMEM((heads, 3 * QROWS, HDIM), bf16),
            pltpu.VMEM((2, heads, HDIM, QROWS), jnp.float32),
            pltpu.VMEM((2, heads, 8, QROWS), jnp.float32),
        ]
        + [pltpu.VMEM((heads, HDIM + STAT, QROWS), bf16)] * 4
        + [pltpu.VMEM((heads, TILE, HDIM), bf16)] * 2
        + [
            pltpu.VMEM((3, STAT, TILE), bf16),
            pltpu.SemaphoreType.DMA((3, heads)),
            pltpu.SemaphoreType.DMA((6, heads)),
            pltpu.SemaphoreType.DMA((6, heads)),
        ],
        compiler_params=pltpu.CompilerParams(
            collective_id=0, has_side_effects=True, vmem_limit_bytes=60 * 1024 * 1024
        ),
    )(queries, keys, values, pad_counts)


def solution(mesh):
    spec = P("frame", "row", None, None)
    return jax.shard_map(
        shards, mesh=mesh, in_specs=(spec, spec, spec, P()), out_specs=spec, check_vma=False
    )
```

```python
import functools

import jax
import jax.numpy as jnp
from jax import lax
from jax.experimental import pallas as pl
from jax.experimental.pallas import tpu as pltpu
from jax.sharding import PartitionSpec as P

HDIM = 128
TILE = 256
QROWS = 128
RT = 4
LOG2E = 1.4426950408889634
AHEAD = 4
Q_AHEAD = 7
LAG = 2
STAT = 16

KV_X, KV_Y, Q_1, Q_2, Q_X, O_1, O_2, O_X = range(8)


def split3(row):
    high = row.astype(jnp.bfloat16).astype(jnp.float32)
    rest = row - high
    middle = rest.astype(jnp.bfloat16).astype(jnp.float32)
    return high, middle, rest - middle


def packed_stats(top, total):
    rows = split3(top) + split3(total)
    at = lax.broadcasted_iota(jnp.int32, (STAT, top.shape[1]), 0)
    out = jnp.zeros((STAT, top.shape[1]), jnp.float32)
    for i, row in enumerate(rows):
        out = jnp.where(at == i, row, out)
    return out.astype(jnp.bfloat16)


def kernel(
    heads, columns, frames, q_hbm, k_hbm, v_hbm, pads, out, kv, qb, part, part_stat,
    to_p, to_x, from_p, from_x, raw_k, raw_v, live_rows, via_o, via_q, local_sem, send_sem, recv_sem,
):
    scale = HDIM ** (-0.5) * LOG2E
    frame, row = lax.axis_index("frame"), lax.axis_index("row")
    rows = RT * columns
    half = 2 * columns
    even = lax.rem(frame, 2) == 0
    r = row // columns
    inner = jnp.logical_or(r == 1, r == 2)
    other_frame = jnp.where(even, frame + 1, frame - 1)
    far_frame = jnp.where(even, frame - 1, frame + 1)
    ahead_frame = lax.rem(jnp.where(even, frame + 2, frame + frames - 2), frames)
    behind_frame = lax.rem(jnp.where(even, frame + frames - 2, frame + 2), frames)
    quarter = columns // 2
    side_base, side_at = (row // half) * half, lax.rem(row, half)
    up_row = side_base + lax.rem(side_at + quarter, half)
    down_row = side_base + lax.rem(side_at + half - quarter, half)
    x_row = lax.rem(row + half, rows)

    across = (other_frame, row)
    onward = (ahead_frame, row)
    cross = (frame, x_row)

    def midway(h, turn):
        return (frame, jnp.where(lax.rem(h + turn, 2) == 0, up_row, down_row))

    def cut(h):
        return pl.ds(pl.multiple_of(h * HDIM, HDIM), HDIM)

    def local_queries(h):
        return pltpu.make_async_copy(q_hbm.at[0, 0, :, cut(h)], qb.at[h, pl.ds(0, QROWS)], local_sem.at[0, h])

    def local_pairs(h):
        return (
            pltpu.make_async_copy(k_hbm.at[0, 0, :, cut(h)], raw_k.at[h], local_sem.at[1, h]),
            pltpu.make_async_copy(v_hbm.at[0, 0, :, cut(h)], raw_v.at[h], local_sem.at[2, h]),
        )

    def remote(kind, h):
        src, dst, device = {
            KV_X: lambda: (kv.at[0, h], kv.at[1, h], across),
            KV_Y: lambda: (kv.at[1, h], kv.at[2, h], onward),
            Q_1: lambda: (qb.at[h, pl.ds(0, QROWS)], via_q.at[h], midway(h, 0)),
            Q_2: lambda: (via_q.at[h], qb.at[h, pl.ds(QROWS, QROWS)], midway(h, 0)),
            Q_X: lambda: (qb.at[h, pl.ds(QROWS, QROWS)], qb.at[h, pl.ds(2 * QROWS, QROWS)], cross),
            O_1: lambda: (to_p.at[h], via_o.at[h], midway(h, 1)),
            O_2: lambda: (via_o.at[h], from_p.at[h], midway(h, 1)),
            O_X: lambda: (to_x.at[h], from_x.at[h], cross),
        }[kind]()
        return pltpu.make_async_remote_copy(
            src_ref=src, dst_ref=dst, send_sem=send_sem.at[kind, h], recv_sem=recv_sem.at[kind, h],
            device_id=device, device_id_type=pl.DeviceIdType.MESH,
        )

    barrier = pltpu.get_barrier_semaphore()
    for device in (across, onward, (behind_frame, row), (frame, up_row), (frame, down_row), cross):
        pl.semaphore_signal(barrier, inc=1, device_id=device, device_id_type=pl.DeviceIdType.MESH)

    @pl.loop(0, heads)
    def _(h):
        for copy in (*local_pairs(h), local_queries(h)):
            copy.start()

    live0 = TILE - pads[frame, row]
    live1 = TILE - pads[other_frame, row]
    far_there = jnp.logical_and(far_frame >= 0, far_frame < frames)
    live2 = jnp.where(far_there, TILE - pads[jnp.clip(far_frame, 0, frames - 1), row], 0)
    lane = lax.broadcasted_iota(jnp.int32, (STAT, TILE), 1)
    for slot, live in enumerate((live0, live1, live2)):
        live_rows[slot] = jnp.where(lane < live, 1.0, 0.0).astype(jnp.bfloat16)

    def send_queries(h):
        local_queries(h).wait()
        remote(Q_1, h).start()

    def prepare(h):
        for copy in local_pairs(h):
            copy.wait()
        at = lax.broadcasted_iota(jnp.int32, (TILE, HDIM), 0)
        keys = raw_k[h].astype(jnp.float32)
        kv[0, h, 0:TILE] = jnp.where(at < live0, keys, keys[0:1]).astype(jnp.bfloat16)
        values = jnp.where(at < live0, raw_v[h].astype(jnp.float32), 0.0)
        for i in range(TILE // HDIM):
            block = jnp.transpose(values[i * HDIM:(i + 1) * HDIM])
            kv[0, h, TILE + i * HDIM:TILE + (i + 1) * HDIM] = block.astype(jnp.bfloat16)

    def attend(h, queries):
        scores = [
            lax.dot_general(
                kv[slot, h, 0:TILE], queries, (((1,), (1,)), ((), ())), preferred_element_type=jnp.float32
            )
            for slot in range(3)
        ]
        top = functools.reduce(jnp.maximum, [jnp.max(s, axis=0, keepdims=True) for s in scores])
        expo = jnp.concatenate([jnp.exp2((s - top) * scale).astype(jnp.bfloat16) for s in scores], axis=0)
        turned = jnp.concatenate(
            [kv[slot, h, TILE + i * HDIM:TILE + (i + 1) * HDIM] for slot in range(3) for i in range(TILE // HDIM)],
            axis=1,
        )
        alive = jnp.concatenate([live_rows[slot] for slot in range(3)], axis=1)
        both = jnp.dot(jnp.concatenate([turned, alive], axis=0), expo, preferred_element_type=jnp.float32)
        return both[0:HDIM], top, both[HDIM:HDIM + 1]

    def packed_into(ref, h, acc, top, total):
        ref[h, 0:HDIM] = acc.astype(jnp.bfloat16)
        ref[h, HDIM:HDIM + STAT] = packed_stats(top, total)

    def keep(which, h, acc, top, total):
        part[which, h] = acc
        part_stat[which, h, 0:1] = top
        part_stat[which, h, 1:2] = total

    def merged(which, h, ref):
        stats = ref[h, HDIM:HDIM + STAT].astype(jnp.float32)
        top2 = stats[0:1] + stats[1:2] + stats[2:3]
        total2 = stats[3:4] + stats[4:5] + stats[5:6]
        top1, total1 = part_stat[which, h, 0:1], part_stat[which, h, 1:2]
        top = jnp.maximum(top1, top2)
        w1, w2 = jnp.exp2((top1 - top) * scale), jnp.exp2((top2 - top) * scale)
        acc = part[which, h] * w1 + ref[h, 0:HDIM].astype(jnp.float32) * w2
        return acc, top, total1 * w1 + total2 * w2

    early, early_queries = min(AHEAD, heads), min(Q_AHEAD, heads)

    @pl.loop(0, early)
    def _(h):
        prepare(h)

    pl.semaphore_wait(barrier, 6)

    @pl.loop(0, early_queries)
    def _(h):
        send_queries(h)

        @pl.when(h < early)
        def _():
            remote(KV_X, h).start()

    def within(at):
        return jnp.logical_and(at >= 0, at < heads)

    def relay_queries(h):
        remote(Q_1, h).wait_recv()
        remote(Q_2, h).start()

    @pl.loop(0, min(3, heads))
    def _(h):
        relay_queries(h)

    def side_queries(h):
        remote(Q_2, h).wait_recv()

        @pl.when(jnp.logical_not(inner))
        def _():
            remote(Q_X, h).start()

    side_queries(0)

    @pl.loop(0, heads + 4 * LAG)
    def _(t):
        @pl.when(within(t))
        def _():
            remote(KV_X, t).wait_recv()
            remote(KV_Y, t).start()

        @pl.when(t + Q_AHEAD < heads)
        def _():
            send_queries(t + Q_AHEAD)

        @pl.when(t + AHEAD < heads)
        def _():
            prepare(t + AHEAD)
            remote(KV_X, t + AHEAD).start()

        @pl.when(t + 3 < heads)
        def _():
            relay_queries(t + 3)

        @pl.when(t + 1 < heads)
        def _():
            side_queries(t + 1)

        @pl.when(within(t - 3 * LAG))
        def _():
            remote(O_1, t - 3 * LAG).wait_recv()
            remote(O_2, t - 3 * LAG).start()

        @pl.when(within(t - LAG))
        def _():
            h = t - LAG
            remote(KV_Y, h).wait_recv()

            @pl.when(jnp.logical_not(far_there))
            def _():
                kv[2, h, 0:TILE] = kv[0, h, 0:TILE]
                kv[2, h, TILE:2 * TILE] = jnp.zeros((TILE, HDIM), jnp.bfloat16)

            @pl.when(inner)
            def _():
                remote(Q_X, h).wait_recv()
                packed_into(to_x, h, *attend(h, qb[h, 2 * QROWS:3 * QROWS]))
                remote(O_X, h).start()

            acc, top, total = attend(h, qb[h, 0:2 * QROWS])
            keep(0, h, acc[:, 0:QROWS], top[:, 0:QROWS], total[:, 0:QROWS])
            for_p = acc[:, QROWS:], top[:, QROWS:], total[:, QROWS:]

            @pl.when(inner)
            def _():
                packed_into(to_p, h, *for_p)
                remote(O_1, h).start()

            @pl.when(jnp.logical_not(inner))
            def _():
                keep(1, h, *for_p)

        @pl.when(jnp.logical_and(jnp.logical_not(inner), within(t - 2 * LAG)))
        def _():
            h = t - 2 * LAG
            remote(O_X, h).wait_recv()
            packed_into(to_p, h, *merged(1, h, from_x))
            remote(O_1, h).start()

        @pl.when(t >= 4 * LAG)
        def _():
            h = t - 4 * LAG
            remote(O_2, h).wait_recv()
            acc, top, total = merged(0, h, from_p)
            done = jnp.transpose(acc / total)
            out[0, 0, :, pl.ds(pl.multiple_of(h * HDIM, HDIM), HDIM)] = done.astype(out.dtype)

    @pl.loop(0, heads)
    def _(h):
        for kind in (KV_X, KV_Y, Q_1, Q_2, O_1, O_2):
            remote(kind, h).wait_send()

        @pl.when(inner)
        def _():
            remote(O_X, h).wait_send()

        @pl.when(jnp.logical_not(inner))
        def _():
            remote(Q_X, h).wait_send()


def shards(queries, keys, values, pad_counts):
    width = queries.shape[-1]
    heads = width // HDIM
    frames, rows = pad_counts.shape
    bf16 = jnp.bfloat16
    return pl.pallas_call(
        functools.partial(kernel, heads, rows // RT, frames),
        out_shape=jax.ShapeDtypeStruct(queries.shape, bf16),
        in_specs=[pl.BlockSpec(memory_space=pl.ANY)] * 3 + [pl.BlockSpec(memory_space=pltpu.SMEM)],
        out_specs=pl.BlockSpec(memory_space=pltpu.VMEM),
        scratch_shapes=[
            pltpu.VMEM((3, heads, 2 * TILE, HDIM), bf16),
            pltpu.VMEM((heads, 3 * QROWS, HDIM), bf16),
            pltpu.VMEM((2, heads, HDIM, QROWS), jnp.float32),
            pltpu.VMEM((2, heads, 8, QROWS), jnp.float32),
        ]
        + [pltpu.VMEM((heads, HDIM + STAT, QROWS), bf16)] * 4
        + [pltpu.VMEM((heads, TILE, HDIM), bf16)] * 2
        + [
            pltpu.VMEM((3, STAT, TILE), bf16),
            pltpu.VMEM((heads, HDIM + STAT, QROWS), bf16),
            pltpu.VMEM((heads, QROWS, HDIM), bf16),
            pltpu.SemaphoreType.DMA((3, heads)),
            pltpu.SemaphoreType.DMA((8, heads)),
            pltpu.SemaphoreType.DMA((8, heads)),
        ],
        compiler_params=pltpu.CompilerParams(
            collective_id=0, has_side_effects=True, vmem_limit_bytes=60 * 1024 * 1024
        ),
    )(queries, keys, values, pad_counts)


def solution(mesh):
    spec = P("frame", "row", None, None)
    return jax.shard_map(
        shards, mesh=mesh, in_specs=(spec, spec, spec, P()), out_specs=spec, check_vma=False
    )
```

```python
import functools

import jax
import jax.numpy as jnp
from jax import lax
from jax.experimental import pallas as pl
from jax.experimental.pallas import tpu as pltpu
from jax.sharding import PartitionSpec as P

HDIM = 128
TILE = 256
QROWS = 128
RT = 4
LOG2E = 1.4426950408889634
AHEAD = 4
LAG = 2
STAT = 16

KV_X, KV_Y, Q_P, Q_X, O_P, O_X = range(6)


def split3(row):
    high = row.astype(jnp.bfloat16).astype(jnp.float32)
    rest = row - high
    middle = rest.astype(jnp.bfloat16).astype(jnp.float32)
    return high, middle, rest - middle


def packed_stats(top, total):
    rows = split3(top) + split3(total)
    at = lax.broadcasted_iota(jnp.int32, (STAT, top.shape[1]), 0)
    out = jnp.zeros((STAT, top.shape[1]), jnp.float32)
    for i, row in enumerate(rows):
        out = jnp.where(at == i, row, out)
    return out.astype(jnp.bfloat16)


def kernel(
    heads, columns, frames, group, q_hbm, k_hbm, v_hbm, pads, out, kv, q_own, q_p, q_x, part, part_stat,
    to_p, to_x, from_p, from_x, raw_k, raw_v, live_rows, local_sem, send_sem, recv_sem,
):
    scale = HDIM ** (-0.5) * LOG2E
    frame, row = lax.axis_index("frame"), lax.axis_index("row")
    rows = RT * columns
    half = 2 * columns
    even = lax.rem(frame, 2) == 0
    r = row // columns
    inner = jnp.logical_or(r == 1, r == 2)
    other_frame = jnp.where(even, frame + 1, frame - 1)
    far_frame = jnp.where(even, frame - 1, frame + 1)
    ahead_frame = lax.rem(jnp.where(even, frame + 2, frame + frames - 2), frames)
    behind_frame = lax.rem(jnp.where(even, frame + frames - 2, frame + 2), frames)
    p_row = (row // half) * half + lax.rem(lax.rem(row, half) + columns, half)
    x_row = lax.rem(row + half, rows)

    across = (other_frame, row)
    onward = (ahead_frame, row)
    side = (frame, p_row)
    cross = (frame, x_row)

    barrier = pltpu.get_barrier_semaphore()
    for device in (across, onward, (behind_frame, row), side, cross):
        pl.semaphore_signal(barrier, inc=1, device_id=device, device_id_type=pl.DeviceIdType.MESH)

    local = (
        pltpu.make_async_copy(k_hbm.at[0, 0], raw_k, local_sem.at[0]),
        pltpu.make_async_copy(v_hbm.at[0, 0], raw_v, local_sem.at[1]),
        pltpu.make_async_copy(q_hbm.at[0, 0], q_own, local_sem.at[2]),
    )
    for copy in local:
        copy.start()

    def cut(h, count=1):
        return pl.ds(pl.multiple_of(h * HDIM, HDIM), count * HDIM)

    def remote(kind, at=None):
        src, dst, device = {
            KV_X: (kv.at[0], kv.at[1], across),
            KV_Y: (kv.at[1], kv.at[2], onward),
            Q_P: (q_own, q_p, side),
            Q_X: (q_p, q_x, cross),
            O_P: (to_p, from_p, side),
            O_X: (to_x, from_x, cross),
        }[kind]
        if at is not None:
            index = (slice(None), cut(at * group, group)) if kind in (Q_P, Q_X) else (at,)
            src, dst = src.at[index], dst.at[index]
        return pltpu.make_async_remote_copy(
            src_ref=src, dst_ref=dst, send_sem=send_sem.at[kind],
            recv_sem=recv_sem.at[kind, 0 if at is None else at],
            device_id=device, device_id_type=pl.DeviceIdType.MESH,
        )

    live0 = TILE - pads[frame, row]
    live1 = TILE - pads[other_frame, row]
    far_there = jnp.logical_and(far_frame >= 0, far_frame < frames)
    live2 = jnp.where(far_there, TILE - pads[jnp.clip(far_frame, 0, frames - 1), row], 0)
    lane = lax.broadcasted_iota(jnp.int32, (STAT, TILE), 1)
    for slot, live in enumerate((live0, live1, live2)):
        live_rows[slot] = jnp.where(lane < live, 1.0, 0.0).astype(jnp.bfloat16)

    def prepare(h):
        at = lax.broadcasted_iota(jnp.int32, (TILE, HDIM), 0)
        keys = raw_k[:, cut(h)].astype(jnp.float32)
        kv[0, h, 0:TILE] = jnp.where(at < live0, keys, keys[0:1]).astype(jnp.bfloat16)
        values = jnp.where(at < live0, raw_v[:, cut(h)].astype(jnp.float32), 0.0)
        for i in range(TILE // HDIM):
            block = jnp.transpose(values[i * HDIM:(i + 1) * HDIM])
            kv[0, h, TILE + i * HDIM:TILE + (i + 1) * HDIM] = block.astype(jnp.bfloat16)

    def attend(h, queries):
        scores = [
            lax.dot_general(
                kv[slot, h, 0:TILE], queries, (((1,), (1,)), ((), ())), preferred_element_type=jnp.float32
            )
            for slot in range(3)
        ]
        top = functools.reduce(jnp.maximum, [jnp.max(s, axis=0, keepdims=True) for s in scores])
        expo = jnp.concatenate([jnp.exp2((s - top) * scale).astype(jnp.bfloat16) for s in scores], axis=0)
        turned = jnp.concatenate(
            [kv[slot, h, TILE + i * HDIM:TILE + (i + 1) * HDIM] for slot in range(3) for i in range(TILE // HDIM)],
            axis=1,
        )
        alive = jnp.concatenate([live_rows[slot] for slot in range(3)], axis=1)
        both = jnp.dot(jnp.concatenate([turned, alive], axis=0), expo, preferred_element_type=jnp.float32)
        return both[0:HDIM], top, both[HDIM:HDIM + 1]

    def packed_into(ref, h, acc, top, total):
        ref[h, 0:HDIM] = acc.astype(jnp.bfloat16)
        ref[h, HDIM:HDIM + STAT] = packed_stats(top, total)

    def keep(which, h, acc, top, total):
        part[which, h] = acc
        part_stat[which, h, 0:1] = top
        part_stat[which, h, 1:2] = total

    def merged(which, h, ref):
        stats = ref[h, HDIM:HDIM + STAT].astype(jnp.float32)
        top2 = stats[0:1] + stats[1:2] + stats[2:3]
        total2 = stats[3:4] + stats[4:5] + stats[5:6]
        top1, total1 = part_stat[which, h, 0:1], part_stat[which, h, 1:2]
        top = jnp.maximum(top1, top2)
        w1, w2 = jnp.exp2((top1 - top) * scale), jnp.exp2((top2 - top) * scale)
        acc = part[which, h] * w1 + ref[h, 0:HDIM].astype(jnp.float32) * w2
        return acc, top, total1 * w1 + total2 * w2

    early, groups = min(AHEAD, heads), heads // group
    for copy in local:
        copy.wait()

    @pl.loop(0, early)
    def _(h):
        prepare(h)

    pl.semaphore_wait(barrier, 5)

    for g in range(min(2, groups)):
        remote(Q_P, g).start()

    @pl.loop(0, early)
    def _(h):
        remote(KV_X, h).start()

    @pl.loop(early, heads)
    def _(h):
        prepare(h)

    def side_queries(g):
        remote(Q_P, g).wait_recv()

        @pl.when(jnp.logical_not(inner))
        def _():
            remote(Q_X, g).start()

    side_queries(0)

    def within(at):
        return jnp.logical_and(at >= 0, at < heads)

    @pl.loop(0, heads + 3 * LAG)
    def _(t):
        @pl.when(within(t))
        def _():
            remote(KV_X, t).wait_recv()
            remote(KV_Y, t).start()

        @pl.when(t + AHEAD < heads)
        def _():
            remote(KV_X, t + AHEAD).start()

        g = t // group
        fresh = t == g * group

        @pl.when(jnp.logical_and(fresh, g + 2 < groups))
        def _():
            remote(Q_P, g + 2).start()

        @pl.when(jnp.logical_and(fresh, g + 1 < groups))
        def _():
            side_queries(g + 1)

        @pl.when(within(t - LAG))
        def _():
            h = t - LAG
            remote(KV_Y, h).wait_recv()

            @pl.when(jnp.logical_not(far_there))
            def _():
                kv[2, h, 0:TILE] = kv[0, h, 0:TILE]
                kv[2, h, TILE:2 * TILE] = jnp.zeros((TILE, HDIM), jnp.bfloat16)

            @pl.when(inner)
            def _():
                @pl.when(h == (h // group) * group)
                def _():
                    remote(Q_X, h // group).wait_recv()

                packed_into(to_x, h, *attend(h, q_x[:, cut(h)]))
                remote(O_X, h).start()

            acc, top, total = attend(h, jnp.concatenate([q_own[:, cut(h)], q_p[:, cut(h)]], axis=0))
            keep(0, h, acc[:, 0:QROWS], top[:, 0:QROWS], total[:, 0:QROWS])
            for_p = acc[:, QROWS:], top[:, QROWS:], total[:, QROWS:]

            @pl.when(inner)
            def _():
                packed_into(to_p, h, *for_p)
                remote(O_P, h).start()

            @pl.when(jnp.logical_not(inner))
            def _():
                keep(1, h, *for_p)

        @pl.when(jnp.logical_and(jnp.logical_not(inner), within(t - 2 * LAG)))
        def _():
            h = t - 2 * LAG
            remote(O_X, h).wait_recv()
            packed_into(to_p, h, *merged(1, h, from_x))
            remote(O_P, h).start()

        @pl.when(t >= 3 * LAG)
        def _():
            h = t - 3 * LAG
            remote(O_P, h).wait_recv()
            acc, top, total = merged(0, h, from_p)
            done = jnp.transpose(acc / total)
            out[0, 0, :, cut(h)] = done.astype(out.dtype)

    for kind in (KV_X, KV_Y, Q_P, O_P):
        remote(kind).wait_send()

    @pl.when(inner)
    def _():
        remote(O_X).wait_send()

    @pl.when(jnp.logical_not(inner))
    def _():
        remote(Q_X).wait_send()


def shards(queries, keys, values, pad_counts):
    width = queries.shape[-1]
    heads = width // HDIM
    frames, rows = pad_counts.shape
    group = 3 if heads % 3 == 0 else 1
    bf16 = jnp.bfloat16
    return pl.pallas_call(
        functools.partial(kernel, heads, rows // RT, frames, group),
        out_shape=jax.ShapeDtypeStruct(queries.shape, bf16),
        in_specs=[pl.BlockSpec(memory_space=pl.ANY)] * 3 + [pl.BlockSpec(memory_space=pltpu.SMEM)],
        out_specs=pl.BlockSpec(memory_space=pltpu.VMEM),
        scratch_shapes=[
            pltpu.VMEM((3, heads, 2 * TILE, HDIM), bf16),
            pltpu.VMEM((QROWS, width), bf16),
            pltpu.VMEM((QROWS, width), bf16),
            pltpu.VMEM((QROWS, width), bf16),
            pltpu.VMEM((2, heads, HDIM, QROWS), jnp.float32),
            pltpu.VMEM((2, heads, 8, QROWS), jnp.float32),
        ]
        + [pltpu.VMEM((heads, HDIM + STAT, QROWS), bf16)] * 4
        + [pltpu.VMEM((TILE, width), bf16)] * 2
        + [
            pltpu.VMEM((3, STAT, TILE), bf16),
            pltpu.SemaphoreType.DMA((3,)),
            pltpu.SemaphoreType.DMA((6,)),
            pltpu.SemaphoreType.DMA((6, heads)),
        ],
        compiler_params=pltpu.CompilerParams(
            collective_id=0, has_side_effects=True, vmem_limit_bytes=60 * 1024 * 1024
        ),
    )(queries, keys, values, pad_counts)


def solution(mesh):
    spec = P("frame", "row", None, None)
    return jax.shard_map(
        shards, mesh=mesh, in_specs=(spec, spec, spec, P()), out_specs=spec, check_vma=False
    )
```

```python
import functools

import jax
import jax.numpy as jnp
from jax import lax
from jax.experimental import pallas as pl
from jax.experimental.pallas import tpu as pltpu
from jax.sharding import PartitionSpec as P

HDIM = 128
TILE = 256
QROWS = 128
RT = 4
LOG2E = 1.4426950408889634
AHEAD = 3
LAG = 3
STAT = 16

KV_X, KV_Y, Q_P, Q_X, O_P, O_X = range(6)


def split3(row):
    high = row.astype(jnp.bfloat16).astype(jnp.float32)
    rest = row - high
    middle = rest.astype(jnp.bfloat16).astype(jnp.float32)
    return high, middle, rest - middle


def packed_stats(top, total):
    rows = split3(top) + split3(total)
    at = lax.broadcasted_iota(jnp.int32, (STAT, top.shape[1]), 0)
    out = jnp.zeros((STAT, top.shape[1]), jnp.float32)
    for i, row in enumerate(rows):
        out = jnp.where(at == i, row, out)
    return out.astype(jnp.bfloat16)


def kernel(
    heads, columns, frames, group, q_hbm, k_hbm, v_hbm, pads, out, kv, q_own, q_p, q_x, part, part_stat,
    to_p, to_x, from_p, from_x, raw_k, raw_v, live_rows, local_sem, send_sem, recv_sem,
):
    scale = HDIM ** (-0.5) * LOG2E
    frame, row = lax.axis_index("frame"), lax.axis_index("row")
    rows = RT * columns
    half = 2 * columns
    even = lax.rem(frame, 2) == 0
    r = row // columns
    inner = jnp.logical_or(r == 1, r == 2)
    other_frame = jnp.where(even, frame + 1, frame - 1)
    far_frame = jnp.where(even, frame - 1, frame + 1)
    ahead_frame = lax.rem(jnp.where(even, frame + 2, frame + frames - 2), frames)
    behind_frame = lax.rem(jnp.where(even, frame + frames - 2, frame + 2), frames)
    p_row = (row // half) * half + lax.rem(lax.rem(row, half) + columns, half)
    x_row = lax.rem(row + half, rows)

    across = (other_frame, row)
    onward = (ahead_frame, row)
    side = (frame, p_row)
    cross = (frame, x_row)

    barrier = pltpu.get_barrier_semaphore()
    for device in (across, onward, (behind_frame, row), side, cross):
        pl.semaphore_signal(barrier, inc=1, device_id=device, device_id_type=pl.DeviceIdType.MESH)

    def local(first, count, part_at):
        span = pl.ds(first * HDIM, count * HDIM)
        pairs = ((q_hbm, q_own), (k_hbm, raw_k), (v_hbm, raw_v))
        return [
            pltpu.make_async_copy(src.at[0, 0, :, span], dst.at[:, span], local_sem.at[part_at, i])
            for i, (src, dst) in enumerate(pairs)
        ]

    local_first, local_rest = local(0, group, 0), local(group, heads - group, 1)
    for copy in local_first + local_rest:
        copy.start()

    def cut(h, count=1):
        return pl.ds(pl.multiple_of(h * HDIM, HDIM), count * HDIM)

    def remote(kind, at=None):
        src, dst, device = {
            KV_X: (kv.at[0], kv.at[1], across),
            KV_Y: (kv.at[1], kv.at[2], onward),
            Q_P: (q_own, q_p, side),
            Q_X: (q_p, q_x, cross),
            O_P: (to_p, from_p, side),
            O_X: (to_x, from_x, cross),
        }[kind]
        if at is not None:
            index = (slice(None), cut(at * group, group)) if kind in (Q_P, Q_X) else (at,)
            src, dst = src.at[index], dst.at[index]
        return pltpu.make_async_remote_copy(
            src_ref=src, dst_ref=dst, send_sem=send_sem.at[kind],
            recv_sem=recv_sem.at[kind, 0 if at is None else at],
            device_id=device, device_id_type=pl.DeviceIdType.MESH,
        )

    live0 = TILE - pads[frame, row]
    live1 = TILE - pads[other_frame, row]
    far_there = jnp.logical_and(far_frame >= 0, far_frame < frames)
    live2 = jnp.where(far_there, TILE - pads[jnp.clip(far_frame, 0, frames - 1), row], 0)
    lane = lax.broadcasted_iota(jnp.int32, (STAT, TILE), 1)
    for slot, live in enumerate((live0, live1, live2)):
        live_rows[slot] = jnp.where(lane < live, 1.0, 0.0).astype(jnp.bfloat16)

    def prepare(h):
        at = lax.broadcasted_iota(jnp.int32, (TILE, HDIM), 0)
        keys = raw_k[:, cut(h)].astype(jnp.float32)
        kv[0, h, 0:TILE] = jnp.where(at < live0, keys, keys[0:1]).astype(jnp.bfloat16)
        values = jnp.where(at < live0, raw_v[:, cut(h)].astype(jnp.float32), 0.0)
        for i in range(TILE // HDIM):
            block = jnp.transpose(values[i * HDIM:(i + 1) * HDIM])
            kv[0, h, TILE + i * HDIM:TILE + (i + 1) * HDIM] = block.astype(jnp.bfloat16)

    def attend(h, queries):
        scores = [
            lax.dot_general(
                kv[slot, h, 0:TILE], queries, (((1,), (1,)), ((), ())), preferred_element_type=jnp.float32
            )
            for slot in range(3)
        ]
        top = functools.reduce(jnp.maximum, [jnp.max(s, axis=0, keepdims=True) for s in scores])
        expo = jnp.concatenate([jnp.exp2((s - top) * scale).astype(jnp.bfloat16) for s in scores], axis=0)
        turned = jnp.concatenate(
            [kv[slot, h, TILE + i * HDIM:TILE + (i + 1) * HDIM] for slot in range(3) for i in range(TILE // HDIM)],
            axis=1,
        )
        alive = jnp.concatenate([live_rows[slot] for slot in range(3)], axis=1)
        both = jnp.dot(jnp.concatenate([turned, alive], axis=0), expo, preferred_element_type=jnp.float32)
        return both[0:HDIM], top, both[HDIM:HDIM + 1]

    def packed_into(ref, h, acc, top, total):
        ref[h, 0:HDIM] = acc.astype(jnp.bfloat16)
        ref[h, HDIM:HDIM + STAT] = packed_stats(top, total)

    def keep(which, h, acc, top, total):
        part[which, h] = acc
        part_stat[which, h, 0:1] = top
        part_stat[which, h, 1:2] = total

    def merged(which, h, ref):
        stats = ref[h, HDIM:HDIM + STAT].astype(jnp.float32)
        top2 = stats[0:1] + stats[1:2] + stats[2:3]
        total2 = stats[3:4] + stats[4:5] + stats[5:6]
        top1, total1 = part_stat[which, h, 0:1], part_stat[which, h, 1:2]
        top = jnp.maximum(top1, top2)
        w1, w2 = jnp.exp2((top1 - top) * scale), jnp.exp2((top2 - top) * scale)
        acc = part[which, h] * w1 + ref[h, 0:HDIM].astype(jnp.float32) * w2
        return acc, top, total1 * w1 + total2 * w2

    early, groups = min(AHEAD, group), heads // group
    pl.semaphore_wait(barrier, 5)
    local_first[0].wait()
    remote(Q_P, 0).start()
    for copy in local_first[1:]:
        copy.wait()

    @pl.loop(0, early)
    def _(h):
        prepare(h)
        remote(KV_X, h).start()

    for copy in local_rest:
        copy.wait()
    for g in range(1, min(2, groups)):
        remote(Q_P, g).start()

    @pl.loop(early, heads)
    def _(h):
        prepare(h)

    for h in range(early, min(AHEAD, heads)):
        remote(KV_X, h).start()

    def side_queries(g):
        remote(Q_P, g).wait_recv()

        @pl.when(jnp.logical_not(inner))
        def _():
            remote(Q_X, g).start()

    side_queries(0)

    def within(at):
        return jnp.logical_and(at >= 0, at < heads)

    @pl.loop(0, heads + 3 * LAG)
    def _(t):
        @pl.when(within(t))
        def _():
            remote(KV_X, t).wait_recv()
            remote(KV_Y, t).start()

        @pl.when(t + AHEAD < heads)
        def _():
            remote(KV_X, t + AHEAD).start()

        g = t // group
        fresh = t == g * group

        @pl.when(jnp.logical_and(fresh, g + 2 < groups))
        def _():
            remote(Q_P, g + 2).start()

        @pl.when(jnp.logical_and(fresh, g + 1 < groups))
        def _():
            side_queries(g + 1)

        @pl.when(within(t - LAG))
        def _():
            h = t - LAG
            remote(KV_Y, h).wait_recv()

            @pl.when(jnp.logical_not(far_there))
            def _():
                kv[2, h, 0:TILE] = kv[0, h, 0:TILE]
                kv[2, h, TILE:2 * TILE] = jnp.zeros((TILE, HDIM), jnp.bfloat16)

            @pl.when(inner)
            def _():
                @pl.when(h == (h // group) * group)
                def _():
                    remote(Q_X, h // group).wait_recv()

                packed_into(to_x, h, *attend(h, q_x[:, cut(h)]))
                remote(O_X, h).start()

            acc, top, total = attend(h, jnp.concatenate([q_own[:, cut(h)], q_p[:, cut(h)]], axis=0))
            keep(0, h, acc[:, 0:QROWS], top[:, 0:QROWS], total[:, 0:QROWS])
            for_p = acc[:, QROWS:], top[:, QROWS:], total[:, QROWS:]

            @pl.when(inner)
            def _():
                packed_into(to_p, h, *for_p)
                remote(O_P, h).start()

            @pl.when(jnp.logical_not(inner))
            def _():
                keep(1, h, *for_p)

        @pl.when(jnp.logical_and(jnp.logical_not(inner), within(t - 2 * LAG)))
        def _():
            h = t - 2 * LAG
            remote(O_X, h).wait_recv()
            packed_into(to_p, h, *merged(1, h, from_x))
            remote(O_P, h).start()

        @pl.when(t >= 3 * LAG)
        def _():
            h = t - 3 * LAG
            remote(O_P, h).wait_recv()
            acc, top, total = merged(0, h, from_p)
            done = jnp.transpose(acc / total)
            out[0, 0, :, cut(h)] = done.astype(out.dtype)

    for kind in (KV_X, KV_Y, Q_P, O_P):
        remote(kind).wait_send()

    @pl.when(inner)
    def _():
        remote(O_X).wait_send()

    @pl.when(jnp.logical_not(inner))
    def _():
        remote(Q_X).wait_send()


def shards(queries, keys, values, pad_counts):
    width = queries.shape[-1]
    heads = width // HDIM
    frames, rows = pad_counts.shape
    group = 3 if heads % 3 == 0 else 1
    bf16 = jnp.bfloat16
    return pl.pallas_call(
        functools.partial(kernel, heads, rows // RT, frames, group),
        out_shape=jax.ShapeDtypeStruct(queries.shape, bf16),
        in_specs=[pl.BlockSpec(memory_space=pl.ANY)] * 3 + [pl.BlockSpec(memory_space=pltpu.SMEM)],
        out_specs=pl.BlockSpec(memory_space=pltpu.VMEM),
        scratch_shapes=[
            pltpu.VMEM((3, heads, 2 * TILE, HDIM), bf16),
            pltpu.VMEM((QROWS, width), bf16),
            pltpu.VMEM((QROWS, width), bf16),
            pltpu.VMEM((QROWS, width), bf16),
            pltpu.VMEM((2, heads, HDIM, QROWS), jnp.float32),
            pltpu.VMEM((2, heads, 8, QROWS), jnp.float32),
        ]
        + [pltpu.VMEM((heads, HDIM + STAT, QROWS), bf16)] * 4
        + [pltpu.VMEM((TILE, width), bf16)] * 2
        + [
            pltpu.VMEM((3, STAT, TILE), bf16),
            pltpu.SemaphoreType.DMA((2, 3)),
            pltpu.SemaphoreType.DMA((6,)),
            pltpu.SemaphoreType.DMA((6, heads)),
        ],
        compiler_params=pltpu.CompilerParams(
            collective_id=0, has_side_effects=True, vmem_limit_bytes=60 * 1024 * 1024
        ),
    )(queries, keys, values, pad_counts)


def solution(mesh):
    spec = P("frame", "row", None, None)
    return jax.shard_map(
        shards, mesh=mesh, in_specs=(spec, spec, spec, P()), out_specs=spec, check_vma=False
    )
```

```python
import functools

import jax
import jax.numpy as jnp
from jax import lax
from jax.experimental import pallas as pl
from jax.experimental.pallas import tpu as pltpu
from jax.sharding import PartitionSpec as P

HDIM = 128
TILE = 256
QROWS = 128
RT = 4
LOG2E = 1.4426950408889634
AHEAD = 4
LAG = 2
STAT = 16

KV_X, KV_Y, Q_P, Q_D, Q_B, Q_C, O_P, O_X, O_Y = range(9)


def split3(row):
    high = row.astype(jnp.bfloat16).astype(jnp.float32)
    rest = row - high
    middle = rest.astype(jnp.bfloat16).astype(jnp.float32)
    return high, middle, rest - middle


def packed_stats(top, total):
    rows = split3(top) + split3(total)
    at = lax.broadcasted_iota(jnp.int32, (STAT, top.shape[1]), 0)
    out = jnp.zeros((STAT, top.shape[1]), jnp.float32)
    for i, row in enumerate(rows):
        out = jnp.where(at == i, row, out)
    return out.astype(jnp.bfloat16)


def kernel(
    heads, columns, frames, group, q_hbm, k_hbm, v_hbm, pads, out, kv, q_own, q_p, q_a, q_b, q_via, part, part_stat,
    to_p, to_x, to_y, from_p, from_x, from_y, raw_k, raw_v, live_rows, local_sem, send_sem, recv_sem,
):
    scale = HDIM ** (-0.5) * LOG2E
    frame, row = lax.axis_index("frame"), lax.axis_index("row")
    rows = RT * columns
    half = 2 * columns
    even = lax.rem(frame, 2) == 0
    r = row // columns
    inner = jnp.logical_or(r == 1, r == 2)
    other_frame = jnp.where(even, frame + 1, frame - 1)
    far_frame = jnp.where(even, frame - 1, frame + 1)
    ahead_frame = lax.rem(jnp.where(even, frame + 2, frame + frames - 2), frames)
    behind_frame = lax.rem(jnp.where(even, frame + frames - 2, frame + 2), frames)
    p_row = (row // half) * half + lax.rem(lax.rem(row, half) + columns, half)
    x_row = lax.rem(row + half, rows)

    across = (other_frame, row)
    onward = (ahead_frame, row)
    side = (frame, p_row)
    behind = (behind_frame, row)
    diagonal = (other_frame, x_row)

    barrier = pltpu.get_barrier_semaphore()
    for device in (across, onward, behind, side, diagonal):
        pl.semaphore_signal(barrier, inc=1, device_id=device, device_id_type=pl.DeviceIdType.MESH)

    def local(first, count, part_at):
        span = pl.ds(first * HDIM, count * HDIM)
        pairs = ((q_hbm, q_own), (k_hbm, raw_k), (v_hbm, raw_v))
        return [
            pltpu.make_async_copy(src.at[0, 0, :, span], dst.at[:, span], local_sem.at[part_at, i])
            for i, (src, dst) in enumerate(pairs)
        ]

    local_first, local_rest = local(0, group, 0), local(group, heads - group, 1)
    for copy in local_first + local_rest:
        copy.start()

    def cut(h, count=1):
        return pl.ds(pl.multiple_of(h * HDIM, HDIM), count * HDIM)

    def remote(kind, at=None):
        src, dst, device = {
            KV_X: (kv.at[0], kv.at[1], across),
            KV_Y: (kv.at[1], kv.at[2], onward),
            Q_P: (q_own, q_p, side),
            Q_D: (q_p, q_a, diagonal),
            Q_B: (q_p, q_via, behind),
            Q_C: (q_via, q_b, diagonal),
            O_P: (to_p, from_p, side),
            O_X: (to_x, from_x, diagonal),
            O_Y: (to_y, from_y, behind),
        }[kind]
        if at is not None:
            index = (slice(None), cut(at * group, group)) if kind in (Q_P, Q_D, Q_B, Q_C) else (at,)
            src, dst = src.at[index], dst.at[index]
        return pltpu.make_async_remote_copy(
            src_ref=src, dst_ref=dst, send_sem=send_sem.at[kind],
            recv_sem=recv_sem.at[kind, 0 if at is None else at],
            device_id=device, device_id_type=pl.DeviceIdType.MESH,
        )

    live0 = TILE - pads[frame, row]
    live1 = TILE - pads[other_frame, row]
    far_there = jnp.logical_and(far_frame >= 0, far_frame < frames)
    live2 = jnp.where(far_there, TILE - pads[jnp.clip(far_frame, 0, frames - 1), row], 0)
    third_frame = jnp.where(even, frame + 2, frame - 2)
    third_there = jnp.logical_and(third_frame >= 0, third_frame < frames)
    lane = lax.broadcasted_iota(jnp.int32, (STAT, TILE), 1)
    for slot, live in enumerate((live0, live1, live2)):
        live_rows[slot] = jnp.where(lane < live, 1.0, 0.0).astype(jnp.bfloat16)

    def prepare(h):
        at = lax.broadcasted_iota(jnp.int32, (TILE, HDIM), 0)
        keys = raw_k[:, cut(h)].astype(jnp.float32)
        kv[0, h, 0:TILE] = jnp.where(at < live0, keys, keys[0:1]).astype(jnp.bfloat16)
        values = jnp.where(at < live0, raw_v[:, cut(h)].astype(jnp.float32), 0.0)
        for i in range(TILE // HDIM):
            block = jnp.transpose(values[i * HDIM:(i + 1) * HDIM])
            kv[0, h, TILE + i * HDIM:TILE + (i + 1) * HDIM] = block.astype(jnp.bfloat16)

    def attend(h, queries, slots):
        scores = [
            lax.dot_general(
                kv[slot, h, 0:TILE], queries, (((1,), (1,)), ((), ())), preferred_element_type=jnp.float32
            )
            for slot in slots
        ]
        top = functools.reduce(jnp.maximum, [jnp.max(s, axis=0, keepdims=True) for s in scores])
        expo = jnp.concatenate([jnp.exp2((s - top) * scale).astype(jnp.bfloat16) for s in scores], axis=0)
        turned = jnp.concatenate(
            [kv[slot, h, TILE + i * HDIM:TILE + (i + 1) * HDIM] for slot in slots for i in range(TILE // HDIM)],
            axis=1,
        )
        alive = jnp.concatenate([live_rows[slot] for slot in slots], axis=1)
        both = jnp.dot(jnp.concatenate([turned, alive], axis=0), expo, preferred_element_type=jnp.float32)
        return both[0:HDIM], top, both[HDIM:HDIM + 1]

    def packed_into(ref, h, acc, top, total):
        ref[h, 0:HDIM] = acc.astype(jnp.bfloat16)
        ref[h, HDIM:HDIM + STAT] = packed_stats(top, total)

    def keep(which, h, acc, top, total):
        part[which, h] = acc
        part_stat[which, h, 0:1] = top
        part_stat[which, h, 1:2] = total

    def kept(which, h):
        return part[which, h], part_stat[which, h, 0:1], part_stat[which, h, 1:2]

    def merged(h, acc1, top1, total1, ref, there=True):
        stats = ref[h, HDIM:HDIM + STAT].astype(jnp.float32)
        top2 = jnp.where(there, stats[0:1] + stats[1:2] + stats[2:3], top1)
        total2 = stats[3:4] + stats[4:5] + stats[5:6]
        top = jnp.maximum(top1, top2)
        w1 = jnp.exp2((top1 - top) * scale)
        w2 = jnp.where(there, jnp.exp2((top2 - top) * scale), 0.0)
        acc = acc1 * w1 + ref[h, 0:HDIM].astype(jnp.float32) * w2
        return acc, top, total1 * w1 + total2 * w2

    early, groups = min(AHEAD, group), heads // group
    pl.semaphore_wait(barrier, 5)
    local_first[0].wait()
    remote(Q_P, 0).start()
    for copy in local_first[1:]:
        copy.wait()

    @pl.loop(0, early)
    def _(h):
        prepare(h)
        remote(KV_X, h).start()

    for copy in local_rest:
        copy.wait()
    for g in range(1, min(2, groups)):
        remote(Q_P, g).start()

    @pl.loop(early, heads)
    def _(h):
        prepare(h)

    for h in range(early, min(AHEAD, heads)):
        remote(KV_X, h).start()

    def side_queries(g):
        remote(Q_P, g).wait_recv()

        @pl.when(jnp.logical_not(inner))
        def _():
            remote(Q_D, g).start()
            remote(Q_B, g).start()

    def relay_queries(g):
        @pl.when(jnp.logical_not(inner))
        def _():
            remote(Q_B, g).wait_recv()
            remote(Q_C, g).start()

    side_queries(0)

    def within(at):
        return jnp.logical_and(at >= 0, at < heads)

    @pl.loop(0, heads + 3 * LAG)
    def _(t):
        @pl.when(within(t))
        def _():
            remote(KV_X, t).wait_recv()
            remote(KV_Y, t).start()

        @pl.when(t + AHEAD < heads)
        def _():
            remote(KV_X, t + AHEAD).start()

        g = t // group
        fresh = t == g * group

        @pl.when(jnp.logical_and(fresh, g + 2 < groups))
        def _():
            remote(Q_P, g + 2).start()

        @pl.when(jnp.logical_and(fresh, g + 1 < groups))
        def _():
            side_queries(g + 1)

        @pl.when(t == 0)
        def _():
            relay_queries(0)

        @pl.when(jnp.logical_and(t == g * group + group // 2, g + 1 < groups))
        def _():
            relay_queries(g + 1)

        def opens(h):
            return h == (h // group) * group

        @pl.when(jnp.logical_and(inner, within(t - 1)))
        def _():
            h = t - 1

            @pl.when(opens(h))
            def _():
                remote(Q_C, h // group).wait_recv()

            packed_into(to_y, h, *attend(h, q_b[:, cut(h)], (0,)))
            remote(O_Y, h).start()

        @pl.when(within(t - LAG))
        def _():
            h = t - LAG
            remote(KV_Y, h).wait_recv()

            @pl.when(jnp.logical_not(far_there))
            def _():
                kv[2, h, 0:TILE] = kv[0, h, 0:TILE]
                kv[2, h, TILE:2 * TILE] = jnp.zeros((TILE, HDIM), jnp.bfloat16)

            queries = jnp.concatenate([q_own[:, cut(h)], q_p[:, cut(h)]], axis=0)
            acc, top, total = attend(h, queries, (0, 1, 2))
            keep(0, h, acc[:, 0:QROWS], top[:, 0:QROWS], total[:, 0:QROWS])
            for_p = acc[:, QROWS:], top[:, QROWS:], total[:, QROWS:]

            @pl.when(inner)
            def _():
                packed_into(to_p, h, *for_p)
                remote(O_P, h).start()

            @pl.when(jnp.logical_not(inner))
            def _():
                keep(1, h, *for_p)

        @pl.when(jnp.logical_and(inner, within(t - 2)))
        def _():
            h = t - 2

            @pl.when(opens(h))
            def _():
                remote(Q_D, h // group).wait_recv()

            near = attend(h, q_a[:, cut(h)], (0, 1))
            remote(O_Y, h).wait_recv()
            packed_into(to_x, h, *merged(h, *near, from_y, third_there))
            remote(O_X, h).start()

        @pl.when(jnp.logical_and(jnp.logical_not(inner), within(t - 2 * LAG)))
        def _():
            h = t - 2 * LAG
            remote(O_X, h).wait_recv()
            packed_into(to_p, h, *merged(h, *kept(1, h), from_x))
            remote(O_P, h).start()

        @pl.when(t >= 3 * LAG)
        def _():
            h = t - 3 * LAG
            remote(O_P, h).wait_recv()
            acc, top, total = merged(h, *kept(0, h), from_p)
            done = jnp.transpose(acc / total)
            out[0, 0, :, cut(h)] = done.astype(out.dtype)

    for kind in (KV_X, KV_Y, Q_P, O_P):
        remote(kind).wait_send()

    @pl.when(inner)
    def _():
        remote(O_X).wait_send()
        remote(O_Y).wait_send()

    @pl.when(jnp.logical_not(inner))
    def _():
        remote(Q_D).wait_send()
        remote(Q_B).wait_send()
        remote(Q_C).wait_send()


def shards(queries, keys, values, pad_counts):
    width = queries.shape[-1]
    heads = width // HDIM
    frames, rows = pad_counts.shape
    group = 3 if heads % 3 == 0 else 1
    bf16 = jnp.bfloat16
    return pl.pallas_call(
        functools.partial(kernel, heads, rows // RT, frames, group),
        out_shape=jax.ShapeDtypeStruct(queries.shape, bf16),
        in_specs=[pl.BlockSpec(memory_space=pl.ANY)] * 3 + [pl.BlockSpec(memory_space=pltpu.SMEM)],
        out_specs=pl.BlockSpec(memory_space=pltpu.VMEM),
        scratch_shapes=[
            pltpu.VMEM((3, heads, 2 * TILE, HDIM), bf16),
        ]
        + [pltpu.VMEM((QROWS, width), bf16)] * 5
        + [
            pltpu.VMEM((2, heads, HDIM, QROWS), jnp.float32),
            pltpu.VMEM((2, heads, 8, QROWS), jnp.float32),
        ]
        + [pltpu.VMEM((heads, HDIM + STAT, QROWS), bf16)] * 6
        + [pltpu.VMEM((TILE, width), bf16)] * 2
        + [
            pltpu.VMEM((3, STAT, TILE), bf16),
            pltpu.SemaphoreType.DMA((2, 3)),
            pltpu.SemaphoreType.DMA((9,)),
            pltpu.SemaphoreType.DMA((9, heads)),
        ],
        compiler_params=pltpu.CompilerParams(
            collective_id=0, has_side_effects=True, vmem_limit_bytes=60 * 1024 * 1024
        ),
    )(queries, keys, values, pad_counts)


def solution(mesh):
    spec = P("frame", "row", None, None)
    return jax.shard_map(
        shards, mesh=mesh, in_specs=(spec, spec, spec, P()), out_specs=spec, check_vma=False
    )
```

```python
import functools

import jax
import jax.numpy as jnp
from jax import lax
from jax.experimental import pallas as pl
from jax.experimental.pallas import tpu as pltpu
from jax.sharding import PartitionSpec as P

HDIM = 128
TILE = 256
QROWS = 128
RT = 4
LOG2E = 1.4426950408889634
AHEAD = 4
LAG = 2
STAT = 16

KV_X, KV_Y, Q_P, Q_X, O_P, O_X = range(6)


def split3(row):
    high = row.astype(jnp.bfloat16).astype(jnp.float32)
    rest = row - high
    middle = rest.astype(jnp.bfloat16).astype(jnp.float32)
    return high, middle, rest - middle


def packed_stats(top, total):
    rows = split3(top) + split3(total)
    at = lax.broadcasted_iota(jnp.int32, (STAT, top.shape[1]), 0)
    out = jnp.zeros((STAT, top.shape[1]), jnp.float32)
    for i, row in enumerate(rows):
        out = jnp.where(at == i, row, out)
    return out.astype(jnp.bfloat16)


def kernel(
    heads, columns, frames, group, q_hbm, k_hbm, v_hbm, pads, out, kv, q_own, q_p, q_x, part, part_stat,
    to_p, to_x, from_p, from_x, raw_k, raw_v, live_rows, local_sem, send_sem, recv_sem,
):
    scale = HDIM ** (-0.5) * LOG2E
    frame, row = lax.axis_index("frame"), lax.axis_index("row")
    rows = RT * columns
    half = 2 * columns
    even = lax.rem(frame, 2) == 0
    r = row // columns
    inner = jnp.logical_or(r == 1, r == 2)
    other_frame = jnp.where(even, frame + 1, frame - 1)
    far_frame = jnp.where(even, frame - 1, frame + 1)
    ahead_frame = lax.rem(jnp.where(even, frame + 2, frame + frames - 2), frames)
    behind_frame = lax.rem(jnp.where(even, frame + frames - 2, frame + 2), frames)
    p_row = (row // half) * half + lax.rem(lax.rem(row, half) + columns, half)
    x_row = lax.rem(row + half, rows)

    across = (other_frame, row)
    onward = (ahead_frame, row)
    side = (frame, p_row)
    cross = (frame, x_row)

    barrier = pltpu.get_barrier_semaphore()
    for device in (across, onward, (behind_frame, row), side, cross):
        pl.semaphore_signal(barrier, inc=1, device_id=device, device_id_type=pl.DeviceIdType.MESH)

    def local(first, count, part_at):
        span = pl.ds(first * HDIM, count * HDIM)
        pairs = ((q_hbm, q_own), (k_hbm, raw_k), (v_hbm, raw_v))
        return [
            pltpu.make_async_copy(src.at[0, 0, :, span], dst.at[:, span], local_sem.at[part_at, i])
            for i, (src, dst) in enumerate(pairs)
        ]

    local_first, local_rest = local(0, group, 0), local(group, heads - group, 1)
    for copy in local_first + local_rest:
        copy.start()

    def cut(h, count=1):
        return pl.ds(pl.multiple_of(h * HDIM, HDIM), count * HDIM)

    def remote(kind, at=None, part_of=None):
        src, dst, device = {
            KV_X: (kv.at[0], kv.at[1], across),
            KV_Y: (kv.at[1], kv.at[2], onward),
            Q_P: (q_own, q_p, side),
            Q_X: (q_p, q_x, cross),
            O_P: (to_p, from_p, side),
            O_X: (to_x, from_x, cross),
        }[kind]
        if at is not None:
            index = (slice(None), cut(at * group, group)) if kind in (Q_P, Q_X) else (at,)
            if part_of is not None:
                index = (at, pl.ds(part_of * TILE, TILE))
            src, dst = src.at[index], dst.at[index]
        return pltpu.make_async_remote_copy(
            src_ref=src, dst_ref=dst, send_sem=send_sem.at[kind],
            recv_sem=recv_sem.at[kind, 0 if at is None else heads if part_of == 1 else at],
            device_id=device, device_id_type=pl.DeviceIdType.MESH,
        )

    live0 = TILE - pads[frame, row]
    live1 = TILE - pads[other_frame, row]
    far_there = jnp.logical_and(far_frame >= 0, far_frame < frames)
    live2 = jnp.where(far_there, TILE - pads[jnp.clip(far_frame, 0, frames - 1), row], 0)
    lane = lax.broadcasted_iota(jnp.int32, (STAT, TILE), 1)
    for slot, live in enumerate((live0, live1, live2)):
        live_rows[slot] = jnp.where(lane < live, 1.0, 0.0).astype(jnp.bfloat16)

    def pairs(h, act):
        last = h == heads - 1

        @pl.when(jnp.logical_not(last))
        def _():
            act(None)

        @pl.when(last)
        def _():
            act(0)
            act(1)

    def send_pairs(h):
        pairs(h, lambda part_of: remote(KV_X, h, part_of).start())

    def pass_pairs(h):
        def act(part_of):
            remote(KV_X, h, part_of).wait_recv()
            remote(KV_Y, h, part_of).start()

        pairs(h, act)

    def prepare(h):
        at = lax.broadcasted_iota(jnp.int32, (TILE, HDIM), 0)
        keys = raw_k[:, cut(h)].astype(jnp.float32)
        kv[0, h, 0:TILE] = jnp.where(at < live0, keys, keys[0:1]).astype(jnp.bfloat16)
        values = jnp.where(at < live0, raw_v[:, cut(h)].astype(jnp.float32), 0.0)
        for i in range(TILE // HDIM):
            block = jnp.transpose(values[i * HDIM:(i + 1) * HDIM])
            kv[0, h, TILE + i * HDIM:TILE + (i + 1) * HDIM] = block.astype(jnp.bfloat16)

    def attend(h, queries):
        scores = [
            lax.dot_general(
                kv[slot, h, 0:TILE], queries, (((1,), (1,)), ((), ())), preferred_element_type=jnp.float32
            )
            for slot in range(3)
        ]
        top = functools.reduce(jnp.maximum, [jnp.max(s, axis=0, keepdims=True) for s in scores])
        expo = jnp.concatenate([jnp.exp2((s - top) * scale).astype(jnp.bfloat16) for s in scores], axis=0)
        turned = jnp.concatenate(
            [kv[slot, h, TILE + i * HDIM:TILE + (i + 1) * HDIM] for slot in range(3) for i in range(TILE // HDIM)],
            axis=1,
        )
        alive = jnp.concatenate([live_rows[slot] for slot in range(3)], axis=1)
        both = jnp.dot(jnp.concatenate([turned, alive], axis=0), expo, preferred_element_type=jnp.float32)
        return both[0:HDIM], top, both[HDIM:HDIM + 1]

    def packed_into(ref, h, acc, top, total):
        ref[h, 0:HDIM] = acc.astype(jnp.bfloat16)
        ref[h, HDIM:HDIM + STAT] = packed_stats(top, total)

    def keep(which, h, acc, top, total):
        part[which, h] = acc
        part_stat[which, h, 0:1] = top
        part_stat[which, h, 1:2] = total

    def merged(which, h, ref):
        stats = ref[h, HDIM:HDIM + STAT].astype(jnp.float32)
        top2 = stats[0:1] + stats[1:2] + stats[2:3]
        total2 = stats[3:4] + stats[4:5] + stats[5:6]
        top1, total1 = part_stat[which, h, 0:1], part_stat[which, h, 1:2]
        top = jnp.maximum(top1, top2)
        w1, w2 = jnp.exp2((top1 - top) * scale), jnp.exp2((top2 - top) * scale)
        acc = part[which, h] * w1 + ref[h, 0:HDIM].astype(jnp.float32) * w2
        return acc, top, total1 * w1 + total2 * w2

    early, groups = min(AHEAD, group), heads // group
    pl.semaphore_wait(barrier, 5)
    local_first[0].wait()
    remote(Q_P, 0).start()
    for copy in local_first[1:]:
        copy.wait()

    @pl.loop(0, early)
    def _(h):
        prepare(h)
        send_pairs(h)

    for copy in local_rest:
        copy.wait()
    for g in range(1, min(2, groups)):
        remote(Q_P, g).start()

    @pl.loop(early, heads)
    def _(h):
        prepare(h)

    for h in range(early, min(AHEAD, heads)):
        send_pairs(jnp.int32(h))

    def side_queries(g):
        remote(Q_P, g).wait_recv()

        @pl.when(jnp.logical_not(inner))
        def _():
            remote(Q_X, g).start()

    side_queries(0)

    def within(at):
        return jnp.logical_and(at >= 0, at < heads)

    @pl.loop(0, heads + 3 * LAG)
    def _(t):
        @pl.when(within(t))
        def _():
            pass_pairs(t)

        @pl.when(t + AHEAD < heads)
        def _():
            send_pairs(t + AHEAD)

        g = t // group
        fresh = t == g * group

        @pl.when(jnp.logical_and(fresh, g + 2 < groups))
        def _():
            remote(Q_P, g + 2).start()

        @pl.when(jnp.logical_and(fresh, g + 1 < groups))
        def _():
            side_queries(g + 1)

        @pl.when(within(t - LAG))
        def _():
            h = t - LAG
            pairs(h, lambda part_of: remote(KV_Y, h, part_of).wait_recv())

            @pl.when(jnp.logical_not(far_there))
            def _():
                kv[2, h, 0:TILE] = kv[0, h, 0:TILE]
                kv[2, h, TILE:2 * TILE] = jnp.zeros((TILE, HDIM), jnp.bfloat16)

            def block(ref):
                return ref[:, cut(h)]

            def columns_of(i, results):
                return [x[:, i * QROWS:(i + 1) * QROWS] for x in results]

            @pl.when(inner)
            def _():
                @pl.when(h == (h // group) * group)
                def _():
                    remote(Q_X, h // group).wait_recv()

                results = attend(h, jnp.concatenate([block(q_own), block(q_p), block(q_x)], axis=0))
                packed_into(to_x, h, *columns_of(2, results))
                remote(O_X, h).start()
                packed_into(to_p, h, *columns_of(1, results))
                remote(O_P, h).start()
                keep(0, h, *columns_of(0, results))

            @pl.when(jnp.logical_not(inner))
            def _():
                results = attend(h, jnp.concatenate([block(q_own), block(q_p)], axis=0))
                keep(0, h, *columns_of(0, results))
                keep(1, h, *columns_of(1, results))

        @pl.when(jnp.logical_and(jnp.logical_not(inner), within(t - 2 * LAG)))
        def _():
            h = t - 2 * LAG
            remote(O_X, h).wait_recv()
            packed_into(to_p, h, *merged(1, h, from_x))
            remote(O_P, h).start()

        @pl.when(t >= 3 * LAG)
        def _():
            h = t - 3 * LAG
            remote(O_P, h).wait_recv()
            acc, top, total = merged(0, h, from_p)
            done = jnp.transpose(acc / total)
            out[0, 0, :, cut(h)] = done.astype(out.dtype)

    for kind in (KV_X, KV_Y, Q_P, O_P):
        remote(kind).wait_send()

    @pl.when(inner)
    def _():
        remote(O_X).wait_send()

    @pl.when(jnp.logical_not(inner))
    def _():
        remote(Q_X).wait_send()


def shards(queries, keys, values, pad_counts):
    width = queries.shape[-1]
    heads = width // HDIM
    frames, rows = pad_counts.shape
    group = 3 if heads % 3 == 0 else 1
    bf16 = jnp.bfloat16
    return pl.pallas_call(
        functools.partial(kernel, heads, rows // RT, frames, group),
        out_shape=jax.ShapeDtypeStruct(queries.shape, bf16),
        in_specs=[pl.BlockSpec(memory_space=pl.ANY)] * 3 + [pl.BlockSpec(memory_space=pltpu.SMEM)],
        out_specs=pl.BlockSpec(memory_space=pltpu.VMEM),
        scratch_shapes=[
            pltpu.VMEM((3, heads, 2 * TILE, HDIM), bf16),
            pltpu.VMEM((QROWS, width), bf16),
            pltpu.VMEM((QROWS, width), bf16),
            pltpu.VMEM((QROWS, width), bf16),
            pltpu.VMEM((2, heads, HDIM, QROWS), jnp.float32),
            pltpu.VMEM((2, heads, 8, QROWS), jnp.float32),
        ]
        + [pltpu.VMEM((heads, HDIM + STAT, QROWS), bf16)] * 4
        + [pltpu.VMEM((TILE, width), bf16)] * 2
        + [
            pltpu.VMEM((3, STAT, TILE), bf16),
            pltpu.SemaphoreType.DMA((2, 3)),
            pltpu.SemaphoreType.DMA((6,)),
            pltpu.SemaphoreType.DMA((6, heads + 1)),
        ],
        compiler_params=pltpu.CompilerParams(
            collective_id=0, has_side_effects=True, vmem_limit_bytes=53 * 1024 * 1024 + 400 * 1024
        ),
    )(queries, keys, values, pad_counts)


def solution(mesh):
    spec = P("frame", "row", None, None)
    return jax.shard_map(
        shards, mesh=mesh, in_specs=(spec, spec, spec, P()), out_specs=spec, check_vma=False
    )
```

```python
import functools

import jax
import jax.numpy as jnp
from jax import lax
from jax.experimental import pallas as pl
from jax.experimental.pallas import tpu as pltpu
from jax.sharding import PartitionSpec as P

HDIM = 128
TILE = 256
QROWS = 128
RT = 4
LOG2E = 1.4426950408889634
AHEAD = 4
LAG = 2
STAT = 16

KV_X, KV_Y, Q_P, Q_X, O_P, O_X = range(6)


def split3(row):
    high = row.astype(jnp.bfloat16).astype(jnp.float32)
    rest = row - high
    middle = rest.astype(jnp.bfloat16).astype(jnp.float32)
    return high, middle, rest - middle


def packed_stats(top, total):
    rows = split3(top) + split3(total)
    at = lax.broadcasted_iota(jnp.int32, (STAT, top.shape[1]), 0)
    out = jnp.zeros((STAT, top.shape[1]), jnp.float32)
    for i, row in enumerate(rows):
        out = jnp.where(at == i, row, out)
    return out.astype(jnp.bfloat16)


def kernel(
    heads, columns, frames, group, q_hbm, k_hbm, v_hbm, pads, out, kv, q_own, q_p, q_x, part, part_stat,
    to_p, to_x, from_p, from_x, raw_k, raw_v, live_rows, local_sem, send_sem, recv_sem,
):
    scale = HDIM ** (-0.5) * LOG2E
    frame, row = lax.axis_index("frame"), lax.axis_index("row")
    rows = RT * columns
    half = 2 * columns
    even = lax.rem(frame, 2) == 0
    r = row // columns
    inner = jnp.logical_or(r == 1, r == 2)
    other_frame = jnp.where(even, frame + 1, frame - 1)
    far_frame = jnp.where(even, frame - 1, frame + 1)
    ahead_frame = lax.rem(jnp.where(even, frame + 2, frame + frames - 2), frames)
    behind_frame = lax.rem(jnp.where(even, frame + frames - 2, frame + 2), frames)
    p_row = (row // half) * half + lax.rem(lax.rem(row, half) + columns, half)
    x_row = lax.rem(row + half, rows)

    across = (other_frame, row)
    onward = (ahead_frame, row)
    side = (frame, p_row)
    cross = (frame, x_row)

    barrier = pltpu.get_barrier_semaphore()
    for device in (across, onward, (behind_frame, row), side, cross):
        pl.semaphore_signal(barrier, inc=1, device_id=device, device_id_type=pl.DeviceIdType.MESH)

    def local(first, count, part_at):
        span = pl.ds(first * HDIM, count * HDIM)
        pairs = ((q_hbm, q_own), (k_hbm, raw_k), (v_hbm, raw_v))
        return [
            pltpu.make_async_copy(src.at[0, 0, :, span], dst.at[:, span], local_sem.at[part_at, i])
            for i, (src, dst) in enumerate(pairs)
        ]

    local_first, local_rest = local(0, group, 0), local(group, heads - group, 1)
    for copy in local_first + local_rest:
        copy.start()

    def cut(h, count=1):
        return pl.ds(pl.multiple_of(h * HDIM, HDIM), count * HDIM)

    def remote(kind, at=None, part_of=None):
        src, dst, device = {
            KV_X: (kv.at[0], kv.at[1], across),
            KV_Y: (kv.at[1], kv.at[2], onward),
            Q_P: (q_own, q_p, side),
            Q_X: (q_p, q_x, cross),
            O_P: (to_p, from_p, side),
            O_X: (to_x, from_x, cross),
        }[kind]
        if at is not None:
            index = (slice(None), cut(at * group, group)) if kind in (Q_P, Q_X) else (at,)
            if part_of is not None:
                index = (at, pl.ds(part_of * TILE, TILE))
            src, dst = src.at[index], dst.at[index]
        return pltpu.make_async_remote_copy(
            src_ref=src, dst_ref=dst, send_sem=send_sem.at[kind],
            recv_sem=recv_sem.at[kind, 0 if at is None else heads + at if part_of == 1 else at],
            device_id=device, device_id_type=pl.DeviceIdType.MESH,
        )

    live0 = TILE - pads[frame, row]
    live1 = TILE - pads[other_frame, row]
    far_there = jnp.logical_and(far_frame >= 0, far_frame < frames)
    live2 = jnp.where(far_there, TILE - pads[jnp.clip(far_frame, 0, frames - 1), row], 0)
    lane = lax.broadcasted_iota(jnp.int32, (STAT, TILE), 1)
    for slot, live in enumerate((live0, live1, live2)):
        live_rows[slot] = jnp.where(lane < live, 1.0, 0.0).astype(jnp.bfloat16)

    def send_pairs(h):
        for part_of in range(2):
            remote(KV_X, h, part_of).start()

    def pass_pairs(h):
        for part_of in range(2):
            remote(KV_X, h, part_of).wait_recv()
            remote(KV_Y, h, part_of).start()

    def prepare(h):
        at = lax.broadcasted_iota(jnp.int32, (TILE, HDIM), 0)
        keys = raw_k[:, cut(h)].astype(jnp.float32)
        kv[0, h, 0:TILE] = jnp.where(at < live0, keys, keys[0:1]).astype(jnp.bfloat16)
        values = jnp.where(at < live0, raw_v[:, cut(h)].astype(jnp.float32), 0.0)
        for i in range(TILE // HDIM):
            block = jnp.transpose(values[i * HDIM:(i + 1) * HDIM])
            kv[0, h, TILE + i * HDIM:TILE + (i + 1) * HDIM] = block.astype(jnp.bfloat16)

    def attend(h, queries):
        scores = [
            lax.dot_general(
                kv[slot, h, 0:TILE], queries, (((1,), (1,)), ((), ())), preferred_element_type=jnp.float32
            )
            for slot in range(3)
        ]
        top = functools.reduce(jnp.maximum, [jnp.max(s, axis=0, keepdims=True) for s in scores])
        expo = jnp.concatenate([jnp.exp2((s - top) * scale).astype(jnp.bfloat16) for s in scores], axis=0)
        turned = jnp.concatenate(
            [kv[slot, h, TILE + i * HDIM:TILE + (i + 1) * HDIM] for slot in range(3) for i in range(TILE // HDIM)],
            axis=1,
        )
        alive = jnp.concatenate([live_rows[slot] for slot in range(3)], axis=1)
        both = jnp.dot(jnp.concatenate([turned, alive], axis=0), expo, preferred_element_type=jnp.float32)
        return both[0:HDIM], top, both[HDIM:HDIM + 1]

    def packed_into(ref, h, acc, top, total):
        ref[h, 0:HDIM] = acc.astype(jnp.bfloat16)
        ref[h, HDIM:HDIM + STAT] = packed_stats(top, total)

    def keep(which, h, acc, top, total):
        part[which, h] = acc
        part_stat[which, h, 0:1] = top
        part_stat[which, h, 1:2] = total

    def merged(which, h, ref):
        stats = ref[h, HDIM:HDIM + STAT].astype(jnp.float32)
        top2 = stats[0:1] + stats[1:2] + stats[2:3]
        total2 = stats[3:4] + stats[4:5] + stats[5:6]
        top1, total1 = part_stat[which, h, 0:1], part_stat[which, h, 1:2]
        top = jnp.maximum(top1, top2)
        w1, w2 = jnp.exp2((top1 - top) * scale), jnp.exp2((top2 - top) * scale)
        acc = part[which, h] * w1 + ref[h, 0:HDIM].astype(jnp.float32) * w2
        return acc, top, total1 * w1 + total2 * w2

    early, groups = min(AHEAD, group), heads // group
    pl.semaphore_wait(barrier, 5)
    local_first[0].wait()
    remote(Q_P, 0).start()
    for copy in local_first[1:]:
        copy.wait()

    @pl.loop(0, early)
    def _(h):
        prepare(h)
        send_pairs(h)

    for copy in local_rest:
        copy.wait()
    for g in range(1, min(2, groups)):
        remote(Q_P, g).start()

    @pl.loop(early, heads)
    def _(h):
        prepare(h)

    for h in range(early, min(AHEAD, heads)):
        send_pairs(h)

    def side_queries(g):
        remote(Q_P, g).wait_recv()

        @pl.when(jnp.logical_not(inner))
        def _():
            remote(Q_X, g).start()

    side_queries(0)

    def within(at):
        return jnp.logical_and(at >= 0, at < heads)

    @pl.loop(0, heads + 3 * LAG)
    def _(t):
        @pl.when(within(t))
        def _():
            pass_pairs(t)

        @pl.when(t + AHEAD < heads)
        def _():
            send_pairs(t + AHEAD)

        g = t // group
        fresh = t == g * group

        @pl.when(jnp.logical_and(fresh, g + 2 < groups))
        def _():
            remote(Q_P, g + 2).start()

        @pl.when(jnp.logical_and(fresh, g + 1 < groups))
        def _():
            side_queries(g + 1)

        @pl.when(within(t - LAG))
        def _():
            h = t - LAG
            for part_of in range(2):
                remote(KV_Y, h, part_of).wait_recv()

            @pl.when(jnp.logical_not(far_there))
            def _():
                kv[2, h, 0:TILE] = kv[0, h, 0:TILE]
                kv[2, h, TILE:2 * TILE] = jnp.zeros((TILE, HDIM), jnp.bfloat16)

            def block(ref):
                return ref[:, cut(h)]

            def columns_of(i, results):
                return [x[:, i * QROWS:(i + 1) * QROWS] for x in results]

            @pl.when(inner)
            def _():
                @pl.when(h == (h // group) * group)
                def _():
                    remote(Q_X, h // group).wait_recv()

                results = attend(h, jnp.concatenate([block(q_own), block(q_p), block(q_x)], axis=0))
                packed_into(to_x, h, *columns_of(2, results))
                remote(O_X, h).start()
                packed_into(to_p, h, *columns_of(1, results))
                remote(O_P, h).start()
                keep(0, h, *columns_of(0, results))

            @pl.when(jnp.logical_not(inner))
            def _():
                results = attend(h, jnp.concatenate([block(q_own), block(q_p)], axis=0))
                keep(0, h, *columns_of(0, results))
                keep(1, h, *columns_of(1, results))

        @pl.when(jnp.logical_and(jnp.logical_not(inner), within(t - 2 * LAG)))
        def _():
            h = t - 2 * LAG
            remote(O_X, h).wait_recv()
            packed_into(to_p, h, *merged(1, h, from_x))
            remote(O_P, h).start()

        @pl.when(t >= 3 * LAG)
        def _():
            h = t - 3 * LAG
            remote(O_P, h).wait_recv()
            acc, top, total = merged(0, h, from_p)
            done = jnp.transpose(acc / total)
            out[0, 0, :, cut(h)] = done.astype(out.dtype)

    for kind in (KV_X, KV_Y, Q_P, O_P):
        remote(kind).wait_send()

    @pl.when(inner)
    def _():
        remote(O_X).wait_send()

    @pl.when(jnp.logical_not(inner))
    def _():
        remote(Q_X).wait_send()


def shards(queries, keys, values, pad_counts):
    width = queries.shape[-1]
    heads = width // HDIM
    frames, rows = pad_counts.shape
    group = 3 if heads % 3 == 0 else 1
    bf16 = jnp.bfloat16
    return pl.pallas_call(
        functools.partial(kernel, heads, rows // RT, frames, group),
        out_shape=jax.ShapeDtypeStruct(queries.shape, bf16),
        in_specs=[pl.BlockSpec(memory_space=pl.ANY)] * 3 + [pl.BlockSpec(memory_space=pltpu.SMEM)],
        out_specs=pl.BlockSpec(memory_space=pltpu.VMEM),
        scratch_shapes=[
            pltpu.VMEM((3, heads, 2 * TILE, HDIM), bf16),
            pltpu.VMEM((QROWS, width), bf16),
            pltpu.VMEM((QROWS, width), bf16),
            pltpu.VMEM((QROWS, width), bf16),
            pltpu.VMEM((2, heads, HDIM, QROWS), jnp.float32),
            pltpu.VMEM((2, heads, 8, QROWS), jnp.float32),
        ]
        + [pltpu.VMEM((heads, HDIM + STAT, QROWS), bf16)] * 4
        + [pltpu.VMEM((TILE, width), bf16)] * 2
        + [
            pltpu.VMEM((3, STAT, TILE), bf16),
            pltpu.SemaphoreType.DMA((2, 3)),
            pltpu.SemaphoreType.DMA((6,)),
            pltpu.SemaphoreType.DMA((6, 2 * heads)),
        ],
        compiler_params=pltpu.CompilerParams(
            collective_id=0, has_side_effects=True, vmem_limit_bytes=53 * 1024 * 1024 + 400 * 1024
        ),
    )(queries, keys, values, pad_counts)


def solution(mesh):
    spec = P("frame", "row", None, None)
    return jax.shard_map(
        shards, mesh=mesh, in_specs=(spec, spec, spec, P()), out_specs=spec, check_vma=False
    )
```

```python
import functools

import jax
import jax.numpy as jnp
from jax import lax
from jax.experimental import pallas as pl
from jax.experimental.pallas import tpu as pltpu
from jax.sharding import PartitionSpec as P

HDIM = 128
TILE = 256
QROWS = 128
RT = 4
LOG2E = 1.4426950408889634
AHEAD = (6, 2)
LAG = 2
STAT = 16

KV_X, KV_Y, Q_P, Q_X, O_P, O_X = range(6)


def split3(row):
    high = row.astype(jnp.bfloat16).astype(jnp.float32)
    rest = row - high
    middle = rest.astype(jnp.bfloat16).astype(jnp.float32)
    return high, middle, rest - middle


def packed_stats(top, total):
    rows = split3(top) + split3(total)
    at = lax.broadcasted_iota(jnp.int32, (STAT, top.shape[1]), 0)
    out = jnp.zeros((STAT, top.shape[1]), jnp.float32)
    for i, row in enumerate(rows):
        out = jnp.where(at == i, row, out)
    return out.astype(jnp.bfloat16)


def kernel(
    heads, columns, frames, group, q_hbm, k_hbm, v_hbm, pads, out, kv, q_own, q_p, q_x, part, part_stat,
    to_p, to_x, from_p, from_x, raw_k, raw_v, live_rows, local_sem, send_sem, recv_sem,
):
    scale = HDIM ** (-0.5) * LOG2E
    frame, row = lax.axis_index("frame"), lax.axis_index("row")
    rows = RT * columns
    half = 2 * columns
    even = lax.rem(frame, 2) == 0
    r = row // columns
    inner = jnp.logical_or(r == 1, r == 2)
    other_frame = jnp.where(even, frame + 1, frame - 1)
    far_frame = jnp.where(even, frame - 1, frame + 1)
    ahead_frame = lax.rem(jnp.where(even, frame + 2, frame + frames - 2), frames)
    behind_frame = lax.rem(jnp.where(even, frame + frames - 2, frame + 2), frames)
    p_row = (row // half) * half + lax.rem(lax.rem(row, half) + columns, half)
    x_row = lax.rem(row + half, rows)

    across = (other_frame, row)
    onward = (ahead_frame, row)
    side = (frame, p_row)
    cross = (frame, x_row)

    barrier = pltpu.get_barrier_semaphore()
    for device in (across, onward, (behind_frame, row), side, cross):
        pl.semaphore_signal(barrier, inc=1, device_id=device, device_id_type=pl.DeviceIdType.MESH)

    def local(first, count, part_at):
        span = pl.ds(first * HDIM, count * HDIM)
        pairs = ((q_hbm, q_own), (k_hbm, raw_k), (v_hbm, raw_v))
        return [
            pltpu.make_async_copy(src.at[0, 0, :, span], dst.at[:, span], local_sem.at[part_at, i])
            for i, (src, dst) in enumerate(pairs)
        ]

    local_first, local_rest = local(0, group, 0), local(group, heads - group, 1)
    for copy in local_first + local_rest:
        copy.start()

    def cut(h, count=1):
        return pl.ds(pl.multiple_of(h * HDIM, HDIM), count * HDIM)

    def remote(kind, at=None, part_of=None):
        src, dst, device = {
            KV_X: (kv.at[0], kv.at[1], across),
            KV_Y: (kv.at[1], kv.at[2], onward),
            Q_P: (q_own, q_p, side),
            Q_X: (q_p, q_x, cross),
            O_P: (to_p, from_p, side),
            O_X: (to_x, from_x, cross),
        }[kind]
        if at is not None:
            index = (slice(None), cut(at * group, group)) if kind in (Q_P, Q_X) else (at,)
            if part_of is not None:
                index = (at, pl.ds(part_of * TILE, TILE))
            src, dst = src.at[index], dst.at[index]
        return pltpu.make_async_remote_copy(
            src_ref=src, dst_ref=dst, send_sem=send_sem.at[kind],
            recv_sem=recv_sem.at[kind, 0 if at is None else heads if part_of == 1 else at],
            device_id=device, device_id_type=pl.DeviceIdType.MESH,
        )

    live0 = TILE - pads[frame, row]
    live1 = TILE - pads[other_frame, row]
    far_there = jnp.logical_and(far_frame >= 0, far_frame < frames)
    live2 = jnp.where(far_there, TILE - pads[jnp.clip(far_frame, 0, frames - 1), row], 0)
    lane = lax.broadcasted_iota(jnp.int32, (STAT, TILE), 1)
    for slot, live in enumerate((live0, live1, live2)):
        live_rows[slot] = jnp.where(lane < live, 1.0, 0.0).astype(jnp.bfloat16)

    def pairs(h, act):
        last = h == heads - 1

        @pl.when(jnp.logical_not(last))
        def _():
            act(None)

        @pl.when(last)
        def _():
            act(0)
            act(1)

    def send_pairs(h):
        pairs(h, lambda part_of: remote(KV_X, h, part_of).start())

    def pass_pairs(h):
        def act(part_of):
            remote(KV_X, h, part_of).wait_recv()
            remote(KV_Y, h, part_of).start()

        pairs(h, act)

    def prepare(h):
        at = lax.broadcasted_iota(jnp.int32, (TILE, HDIM), 0)
        keys = raw_k[:, cut(h)].astype(jnp.float32)
        kv[0, h, 0:TILE] = jnp.where(at < live0, keys, keys[0:1]).astype(jnp.bfloat16)
        values = jnp.where(at < live0, raw_v[:, cut(h)].astype(jnp.float32), 0.0)
        for i in range(TILE // HDIM):
            block = jnp.transpose(values[i * HDIM:(i + 1) * HDIM])
            kv[0, h, TILE + i * HDIM:TILE + (i + 1) * HDIM] = block.astype(jnp.bfloat16)

    def attend(h, queries):
        scores = [
            lax.dot_general(
                kv[slot, h, 0:TILE], queries, (((1,), (1,)), ((), ())), preferred_element_type=jnp.float32
            )
            for slot in range(3)
        ]
        top = functools.reduce(jnp.maximum, [jnp.max(s, axis=0, keepdims=True) for s in scores])
        expo = jnp.concatenate([jnp.exp2((s - top) * scale).astype(jnp.bfloat16) for s in scores], axis=0)
        turned = jnp.concatenate(
            [kv[slot, h, TILE + i * HDIM:TILE + (i + 1) * HDIM] for slot in range(3) for i in range(TILE // HDIM)],
            axis=1,
        )
        alive = jnp.concatenate([live_rows[slot] for slot in range(3)], axis=1)
        both = jnp.dot(jnp.concatenate([turned, alive], axis=0), expo, preferred_element_type=jnp.float32)
        return both[0:HDIM], top, both[HDIM:HDIM + 1]

    def packed_into(ref, h, acc, top, total):
        ref[h, 0:HDIM] = acc.astype(jnp.bfloat16)
        ref[h, HDIM:HDIM + STAT] = packed_stats(top, total)

    def keep(which, h, acc, top, total):
        part[which, h] = acc
        part_stat[which, h, 0:1] = top
        part_stat[which, h, 1:2] = total

    def merged(which, h, ref):
        stats = ref[h, HDIM:HDIM + STAT].astype(jnp.float32)
        top2 = stats[0:1] + stats[1:2] + stats[2:3]
        total2 = stats[3:4] + stats[4:5] + stats[5:6]
        top1, total1 = part_stat[which, h, 0:1], part_stat[which, h, 1:2]
        top = jnp.maximum(top1, top2)
        w1, w2 = jnp.exp2((top1 - top) * scale), jnp.exp2((top2 - top) * scale)
        acc = part[which, h] * w1 + ref[h, 0:HDIM].astype(jnp.float32) * w2
        return acc, top, total1 * w1 + total2 * w2

    early, groups = min(max(AHEAD), group), heads // group
    window = jnp.where(lax.rem(row, 2) == 0, AHEAD[0], AHEAD[1])
    pl.semaphore_wait(barrier, 5)
    local_first[0].wait()
    remote(Q_P, 0).start()
    for copy in local_first[1:]:
        copy.wait()

    @pl.loop(0, early)
    def _(h):
        prepare(h)

        @pl.when(h < window)
        def _():
            send_pairs(h)

    for copy in local_rest:
        copy.wait()
    for g in range(1, min(2, groups)):
        remote(Q_P, g).start()

    @pl.loop(early, heads)
    def _(h):
        prepare(h)

    @pl.loop(early, min(max(AHEAD), heads))
    def _(h):
        @pl.when(h < window)
        def _():
            send_pairs(h)

    def side_queries(g):
        remote(Q_P, g).wait_recv()

        @pl.when(jnp.logical_not(inner))
        def _():
            remote(Q_X, g).start()

    side_queries(0)

    def within(at):
        return jnp.logical_and(at >= 0, at < heads)

    @pl.loop(0, heads + 3 * LAG)
    def _(t):
        @pl.when(within(t))
        def _():
            pass_pairs(t)

        @pl.when(t + window < heads)
        def _():
            send_pairs(t + window)

        g = t // group
        fresh = t == g * group

        @pl.when(jnp.logical_and(fresh, g + 2 < groups))
        def _():
            remote(Q_P, g + 2).start()

        @pl.when(jnp.logical_and(fresh, g + 1 < groups))
        def _():
            side_queries(g + 1)

        @pl.when(within(t - LAG))
        def _():
            h = t - LAG
            pairs(h, lambda part_of: remote(KV_Y, h, part_of).wait_recv())

            @pl.when(jnp.logical_not(far_there))
            def _():
                kv[2, h, 0:TILE] = kv[0, h, 0:TILE]
                kv[2, h, TILE:2 * TILE] = jnp.zeros((TILE, HDIM), jnp.bfloat16)

            def block(ref):
                return ref[:, cut(h)]

            def columns_of(i, results):
                return [x[:, i * QROWS:(i + 1) * QROWS] for x in results]

            @pl.when(inner)
            def _():
                @pl.when(h == (h // group) * group)
                def _():
                    remote(Q_X, h // group).wait_recv()

                results = attend(h, jnp.concatenate([block(q_own), block(q_p), block(q_x)], axis=0))
                packed_into(to_x, h, *columns_of(2, results))
                remote(O_X, h).start()
                packed_into(to_p, h, *columns_of(1, results))
                remote(O_P, h).start()
                keep(0, h, *columns_of(0, results))

            @pl.when(jnp.logical_not(inner))
            def _():
                results = attend(h, jnp.concatenate([block(q_own), block(q_p)], axis=0))
                keep(0, h, *columns_of(0, results))
                keep(1, h, *columns_of(1, results))

        @pl.when(jnp.logical_and(jnp.logical_not(inner), within(t - 2 * LAG)))
        def _():
            h = t - 2 * LAG
            remote(O_X, h).wait_recv()
            packed_into(to_p, h, *merged(1, h, from_x))
            remote(O_P, h).start()

        @pl.when(t >= 3 * LAG)
        def _():
            h = t - 3 * LAG
            remote(O_P, h).wait_recv()
            acc, top, total = merged(0, h, from_p)
            done = jnp.transpose(acc / total)
            out[0, 0, :, cut(h)] = done.astype(out.dtype)

    for kind in (KV_X, KV_Y, Q_P, O_P):
        remote(kind).wait_send()

    @pl.when(inner)
    def _():
        remote(O_X).wait_send()

    @pl.when(jnp.logical_not(inner))
    def _():
        remote(Q_X).wait_send()


def shards(queries, keys, values, pad_counts):
    width = queries.shape[-1]
    heads = width // HDIM
    frames, rows = pad_counts.shape
    group = 3 if heads % 3 == 0 else 1
    bf16 = jnp.bfloat16
    return pl.pallas_call(
        functools.partial(kernel, heads, rows // RT, frames, group),
        out_shape=jax.ShapeDtypeStruct(queries.shape, bf16),
        in_specs=[pl.BlockSpec(memory_space=pl.ANY)] * 3 + [pl.BlockSpec(memory_space=pltpu.SMEM)],
        out_specs=pl.BlockSpec(memory_space=pltpu.VMEM),
        scratch_shapes=[
            pltpu.VMEM((3, heads, 2 * TILE, HDIM), bf16),
            pltpu.VMEM((QROWS, width), bf16),
            pltpu.VMEM((QROWS, width), bf16),
            pltpu.VMEM((QROWS, width), bf16),
            pltpu.VMEM((2, heads, HDIM, QROWS), jnp.float32),
            pltpu.VMEM((2, heads, 8, QROWS), jnp.float32),
        ]
        + [pltpu.VMEM((heads, HDIM + STAT, QROWS), bf16)] * 4
        + [pltpu.VMEM((TILE, width), bf16)] * 2
        + [
            pltpu.VMEM((3, STAT, TILE), bf16),
            pltpu.SemaphoreType.DMA((2, 3)),
            pltpu.SemaphoreType.DMA((6,)),
            pltpu.SemaphoreType.DMA((6, heads + 1)),
        ],
        compiler_params=pltpu.CompilerParams(
            collective_id=0, has_side_effects=True, vmem_limit_bytes=53 * 1024 * 1024 + 400 * 1024
        ),
    )(queries, keys, values, pad_counts)


def solution(mesh):
    spec = P("frame", "row", None, None)
    return jax.shard_map(
        shards, mesh=mesh, in_specs=(spec, spec, spec, P()), out_specs=spec, check_vma=False
    )
```
